32 devices in a mesh: replica: 4 (over x, core), fsdp: 8 (over z, y).
Axes of the slice: x: 2, y: 2, z: 4, core: 2. Of those that a mesh axis runs over, the one named last changes fastest.
Arguments:
- tokens: bfloat16 [32, 128, 768], P(('replica', 'fsdp')), may hold values from -6 to 6
- encoded: bfloat16 [32, 2, 64, 768], P(('replica', 'fsdp')), may hold values from -6 to 6
- lengths: int32 [32, 2], P(('replica', 'fsdp')), may hold values from 16 to 112, as said below
- cotangent: bfloat16 [32, 128, 768], P(('replica', 'fsdp')), may hold values from -6 to 6
- norm_self: bfloat16 [768], P('fsdp'), may hold values from 0.5 to 1.5
- q_self: bfloat16 [768, 768], P('fsdp'), may hold values from -0.109375 to 0.109375
- k_self: bfloat16 [768, 768], P('fsdp'), may hold values from -0.109375 to 0.109375
- v_self: bfloat16 [768, 768], P('fsdp'), may hold values from -0.21875 to 0.21875
- o_self: bfloat16 [768, 768], P('fsdp'), may hold values from -0.875 to 0.875
- bias_table: bfloat16 [32, 12], P('fsdp'), may hold values from -4 to 4
- norm_cross: bfloat16 [768], P('fsdp'), may hold values from 0.5 to 1.5
- q_cross: bfloat16 [768, 768], P('fsdp'), may hold values from -0.109375 to 0.109375
- k_cross: bfloat16 [768, 768], P('fsdp'), may hold values from -0.109375 to 0.109375
- v_cross: bfloat16 [768, 768], P('fsdp'), may hold values from -0.21875 to 0.21875
- o_cross: bfloat16 [768, 768], P('fsdp'), may hold values from -0.875 to 0.875
- norm_ff: bfloat16 [768], P('fsdp'), may hold values from 0.5 to 1.5
- wi_gate: bfloat16 [768, 2048], P('fsdp'), may hold values from -0.21875 to 0.21875
- wi_up: bfloat16 [768, 2048], P('fsdp'), may hold values from -0.21875 to 0.21875
- wo_ff: bfloat16 [2048, 768], P('fsdp'), may hold values from -0.125 to 0.125
Outputs:
- mixed: bfloat16 [32, 128, 768], P(('replica', 'fsdp'))
- tokens_grad: float32 [32, 128, 768], P(('replica', 'fsdp'))
- encoded_grad: float32 [32, 2, 64, 768], P(('replica', 'fsdp'))
- norm_self_grad: float32 [768], P('fsdp')
- q_self_grad: float32 [768, 768], P('fsdp')
- k_self_grad: float32 [768, 768], P('fsdp')
- v_self_grad: float32 [768, 768], P('fsdp')
- o_self_grad: float32 [768, 768], P('fsdp')
- bias_table_grad: float32 [32, 12], P('fsdp')
- norm_cross_grad: float32 [768], P('fsdp')
- q_cross_grad: float32 [768, 768], P('fsdp')
- k_cross_grad: float32 [768, 768], P('fsdp')
- v_cross_grad: float32 [768, 768], P('fsdp')
- o_cross_grad: float32 [768, 768], P('fsdp')
- norm_ff_grad: float32 [768], P('fsdp')
- wi_gate_grad: float32 [768, 2048], P('fsdp')
- wi_up_grad: float32 [768, 2048], P('fsdp')
- wo_ff_grad: float32 [2048, 768], P('fsdp')
The draws below stay inside these ranges and needn't reach their ends.
Inputs may be any that keep to these rules, and one draw needn't show every extreme that they name: Each slot holds two sequences packed from its first row; their lengths sum to at most 128, and some slot is filled to 128 in every draw.
All inputs are finite; a program needn't handle non-finite values.
Results may differ from the reference program's by a relative error of at most 0.025.
The reference program's roundings to bfloat16 on the way count: a program that leaves them out, or rounds other values in their place, can miss the bound.
Values may be sent and summed in bfloat16 or wider, within the bound.
No kernel may reach another device: no remote copies, remote signals or barrier semaphores. Data moves between devices by JAX's collectives and lax.ppermute only.
A program may use at most 128 MiB of HBM per device.

```python
import math
import jax
import jax.numpy as jnp
import numpy as np
from jax import lax

D = 768
HEADS = 12
DH = 64
FF = 2048
BUCKETS = 32
CAP = 128
ENC = 64
SEQ_DEV = 2
SLOTS = 32


def draw_lengths(key, part):
    key = jax.random.fold_in(key, 11)
    key_total, key_first, key_pick = jax.random.split(key, 3)
    shortest = CAP // 8
    totals = jax.random.randint(key_total, (SLOTS,), CAP // 2, CAP + 1)
    picked = jax.random.randint(key_pick, (), 0, SLOTS)
    chosen = lax.iota(jnp.int32, SLOTS) == picked
    totals = jnp.where(chosen, CAP, totals)
    firsts = jax.random.randint(key_first, (SLOTS,), shortest, totals - shortest + 1)
    firsts = jnp.where(chosen, CAP - shortest, firsts)
    return jnp.stack([firsts, totals - firsts], axis=1).astype(jnp.int32)


def block_levels(key, dims, cuts, smallest, top_value):
    factor_of, own = 1.0, jax.random.fold_in(key, 6)
    for dim, parts in cuts:
        heights = jnp.exp(jax.random.uniform(jax.random.fold_in(own, dim), (parts,), jnp.float32, smallest / len(cuts), top_value / len(cuts)))
        factor_of = factor_of * jnp.repeat(heights, dims[dim] // parts).reshape([-1 if axis == dim else 1 for axis in range(len(dims))])
    return factor_of


def centred(stream_key, dims, scale, bound, cuts=(), dtype=jnp.bfloat16):
    entries = scale * jax.random.normal(stream_key, dims, jnp.float32)
    if cuts:
        entries = entries * block_levels(stream_key, dims, cuts, -0.22, 0.18)
    return jnp.clip(entries, -bound, bound).astype(dtype)


def setup_inputs(seed: int = 0) -> dict:
    arg_keys = jax.random.split(jax.random.key(seed), 20)
    tokens = centred(arg_keys[0], (SLOTS, CAP, D), 1.0, 6.0, ((0, 32),))
    encoded = centred(arg_keys[1], (SLOTS, SEQ_DEV, ENC, D), 1.0, 6.0, ((0, 32),))
    lengths = draw_lengths(jax.random.fold_in(arg_keys[19], 71), 0)
    cotangent = centred(arg_keys[3], (SLOTS, CAP, D), 1.0, 6.0, ((0, 32),))
    norm_self = jnp.clip(1.0 + 0.1 * jax.random.normal(arg_keys[4], (D,), jnp.float32), 0.5, 1.5).astype(jnp.bfloat16)
    q_self = centred(arg_keys[5], (D, D), (4 * D) ** -0.5, 0.109375, ((0, 8),))
    k_self = centred(arg_keys[6], (D, D), (4 * D) ** -0.5, 0.109375, ((0, 8),))
    v_self = centred(arg_keys[7], (D, D), D ** -0.5, 0.21875, ((0, 8),))
    o_self = centred(arg_keys[8], (D, D), (D // 16) ** -0.5, 0.875, ((0, 8),))
    bias_table = centred(arg_keys[9], (BUCKETS, HEADS), 1.0, 4.0, ((0, 8),))
    norm_cross = jnp.clip(1.0 + 0.1 * jax.random.normal(arg_keys[10], (D,), jnp.float32), 0.5, 1.5).astype(jnp.bfloat16)
    q_cross = centred(arg_keys[11], (D, D), (4 * D) ** -0.5, 0.109375, ((0, 8),))
    k_cross = centred(arg_keys[12], (D, D), (4 * D) ** -0.5, 0.109375, ((0, 8),))
    v_cross = centred(arg_keys[13], (D, D), D ** -0.5, 0.21875, ((0, 8),))
    o_cross = centred(arg_keys[14], (D, D), (D // 16) ** -0.5, 0.875, ((0, 8),))
    norm_ff = jnp.clip(1.0 + 0.1 * jax.random.normal(arg_keys[15], (D,), jnp.float32), 0.5, 1.5).astype(jnp.bfloat16)
    wi_gate = centred(arg_keys[16], (D, FF), D ** -0.5, 0.21875, ((0, 8),))
    wi_up = centred(arg_keys[17], (D, FF), D ** -0.5, 0.21875, ((0, 8),))
    wo_ff = centred(arg_keys[18], (FF, D), FF ** -0.5, 0.125, ((0, 8),))
    return {"tokens": tokens, "encoded": encoded, "lengths": lengths, "cotangent": cotangent, "norm_self": norm_self, "q_self": q_self, "k_self": k_self, "v_self": v_self, "o_self": o_self, "bias_table": bias_table, "norm_cross": norm_cross, "q_cross": q_cross, "k_cross": k_cross, "v_cross": v_cross, "o_cross": o_cross, "norm_ff": norm_ff, "wi_gate": wi_gate, "wi_up": wi_up, "wo_ff": wo_ff}


EPS = 1e-06
NEG = -1e+30
bucket_edges = np.array([math.ceil(16 * 8 ** (k / 16)) for k in range(1, 16)], np.int32)

@jax.custom_vjp
def low(v):
    return lax.optimization_barrier(v.astype(jnp.bfloat16)).astype(jnp.float32)

@jax.custom_vjp
def low_back(v):
    return v

def low_keep(v):
    return (low(v), None)

def low_pass(kept, grad):
    return (grad,)

def back_keep(v):
    return (v, None)

def back_low(kept, grad):
    return (low(grad),)
low.defvjp(low_keep, low_pass)
low_back.defvjp(back_keep, back_low)

def bucket_of(offset):
    distance = jnp.maximum(offset, 0)
    counted = lax.optimization_barrier(jnp.sum((distance[..., None] >= jnp.asarray(bucket_edges)).astype(jnp.int32), axis=-1))
    return jnp.where(distance < 16, distance, 16 + counted)

def segment_ids(seq_lens, row_count):
    places = lax.iota(jnp.int32, row_count)
    bounds = jnp.cumsum(seq_lens)
    return lax.optimization_barrier(jnp.sum((places[:, None] >= bounds[None, :]).astype(jnp.int32), axis=1))

def rms_scale(values, gain_vec):
    return values * lax.rsqrt(lax.optimization_barrier(jnp.mean(values * values, axis=-1, keepdims=True)) + EPS) * gain_vec

def gelu_mix(gate_pre, up_pre):
    return jax.nn.gelu(gate_pre, approximate=True) * up_pre

def product(left_side, right_side):
    return jnp.dot(left_side, right_side, precision=lax.Precision.HIGHEST, preferred_element_type=jnp.float32)

def split_heads(values):
    return values.reshape(values.shape[0], HEADS, DH)

def attention(queries, key_rows, values, allowed, bias):
    scores = jnp.einsum('qhd,khd->hqk', queries, key_rows, precision=lax.Precision.HIGHEST)
    if bias is not None:
        scores = scores + bias
    scores = low_back(scores)
    masked = jnp.where(allowed[None], scores, NEG)
    summit = lax.optimization_barrier(jnp.max(masked, axis=-1, keepdims=True))
    raised = jnp.exp(masked - summit)
    weights_soft = low(raised / lax.optimization_barrier(jnp.sum(raised, axis=-1, keepdims=True)))
    return jnp.einsum('hqk,khd->qhd', weights_soft, values, precision=lax.Precision.HIGHEST)

def slot_layer(params, inputs, encoder, seq_lens):
    norm_one, query_one, key_one, value_one, out_one, table_full, norm_two, query_two, key_two, value_two, out_two, norm_three, gate_full, up_full, down_full = params
    row_count = inputs.shape[0]
    feature_count = inputs.shape[1]
    enc_rows = encoder.shape[0]
    segment = segment_ids(seq_lens, row_count)
    live_rows = (segment < SEQ_DEV).astype(jnp.float32)[:, None]
    places = lax.iota(jnp.int32, row_count)
    self_ok = (segment[:, None] == segment[None, :]) & (places[:, None] >= places[None, :])
    bias = jnp.transpose(table_full[bucket_of(places[:, None] - places[None, :])], (2, 0, 1))
    cross_ok = jnp.minimum(segment, SEQ_DEV - 1)[:, None] == (lax.iota(jnp.int32, enc_rows) // ENC)[None, :]
    normed_one = low(rms_scale(inputs, norm_one))
    queries = low_back(low(product(normed_one, query_one)))
    key_self = low_back(low(product(normed_one, key_one)))
    value_self = low_back(low(product(normed_one, value_one)))
    attn_one = attention(split_heads(queries), split_heads(key_self), split_heads(value_self), self_ok, bias)
    attn_one = low_back(low(attn_one.reshape(row_count, feature_count)))
    hidden_one = inputs + live_rows * low_back(product(attn_one, out_one))
    normed_two = low(rms_scale(hidden_one, norm_two))
    query_cross = low_back(low(product(normed_two, query_two)))
    key_cross = low_back(low(product(encoder, key_two)))
    value_cross = low_back(low(product(encoder, value_two)))
    attn_two = attention(split_heads(query_cross), split_heads(key_cross), split_heads(value_cross), cross_ok, None)
    attn_two = low_back(low(attn_two.reshape(row_count, feature_count)))
    hidden_two = hidden_one + live_rows * low_back(product(attn_two, out_two))
    normed_three = low(rms_scale(hidden_two, norm_three))
    gate_pre = low_back(product(normed_three, gate_full))
    up_pre = low_back(product(normed_three, up_full))
    activ = low(gelu_mix(gate_pre, up_pre))
    return hidden_two + live_rows * low_back(product(activ, down_full))

def reference(tokens, encoded, lengths, cotangent, norm_self, q_self, k_self, v_self, o_self, bias_table, norm_cross, q_cross, k_cross, v_cross, o_cross, norm_ff, wi_gate, wi_up, wo_ff):
    params = tuple((weight.astype(jnp.float32) for weight in (norm_self, q_self, k_self, v_self, o_self, bias_table, norm_cross, q_cross, k_cross, v_cross, o_cross, norm_ff, wi_gate, wi_up, wo_ff)))
    inputs_all = tokens.astype(jnp.float32)
    encoder_all = encoded.astype(jnp.float32).reshape(encoded.shape[0], -1, encoded.shape[-1])
    layer_step = jax.checkpoint(slot_layer)

    def forward(weights_all, token_rows, encoder_rows):

        def slot_step(sliced):
            return layer_step(weights_all, sliced[0], sliced[1], sliced[2])
        return lax.map(slot_step, (token_rows, encoder_rows, lengths))
    result, pullback = jax.vjp(forward, params, inputs_all, encoder_all)
    grad_params, grad_inputs, grad_encoder = pullback(cotangent.astype(jnp.float32))
    return (result.astype(jnp.bfloat16), grad_inputs, grad_encoder.reshape(encoded.shape), grad_params[0], grad_params[1], grad_params[2], grad_params[3], grad_params[4], grad_params[5], grad_params[6], grad_params[7], grad_params[8], grad_params[9], grad_params[10], grad_params[11], grad_params[12], grad_params[13], grad_params[14])
```

```python
import functools
import math

import jax
import jax.numpy as jnp
import numpy as np
from jax import lax
from jax.experimental import pallas as pl
from jax.experimental.pallas import tpu as pltpu
from jax.sharding import PartitionSpec as P

HEADS = 12
PAIR = 128
EPS = 1e-06
NEG = -1e30
SQRT_2_PI = math.sqrt(2 / math.pi)
bucket_edges = np.array([math.ceil(16 * 8 ** (k / 16)) for k in range(1, 16)], np.int32)

F32 = jnp.float32
BF16 = jnp.bfloat16
VMEM = pl.BlockSpec(memory_space=pltpu.VMEM)
SMEM = pl.BlockSpec(memory_space=pltpu.SMEM)
ANY = pl.BlockSpec(memory_space=pl.ANY)


def params(limit=56):
    return pltpu.CompilerParams(vmem_limit_bytes=limit * 1024 * 1024)


def cost(flops, nbytes):
    return pl.CostEstimate(flops=flops, bytes_accessed=nbytes, transcendentals=0)


def bucket_of(offset):
    distance = jnp.maximum(offset, 0)
    counted = jnp.sum((distance[..., None] >= jnp.asarray(bucket_edges)).astype(jnp.int32), axis=-1)
    return jnp.where(distance < 16, distance, 16 + counted)


def mm(left, right):
    return jnp.dot(left, right, preferred_element_type=F32)


def mm_nt(left, right):
    return lax.dot_general(left, right, (((1,), (1,)), ((), ())), preferred_element_type=F32)


def mm_tn(left, right):
    return lax.dot_general(left, right, (((0,), (0,)), ((), ())), preferred_element_type=F32)


def choose(flag, left, right):
    return lax.select(flag, left, right)


def segments(bounds, shape, axis):
    place = lax.broadcasted_iota(jnp.int32, shape, axis)
    segment = jnp.zeros(shape, jnp.int32)
    for bound in bounds:
        segment = segment + (place >= bound).astype(jnp.int32)
    return segment


def read_bounds(info, seq_count):
    bounds, total = [], 0
    for index in range(seq_count):
        total = total + info[4 + index]
        bounds.append(total)
    return bounds


def rms_parts(values, gain):
    scale = lax.rsqrt(jnp.mean(values * values, axis=-1, keepdims=True) + EPS)
    return scale, (values * scale * gain).astype(BF16)


def rms_back(values, gain, grad):
    scale = lax.rsqrt(jnp.mean(values * values, axis=-1, keepdims=True) + EPS)
    weighted = grad * gain
    inner = jnp.mean(weighted * values, axis=-1, keepdims=True)
    grad_values = scale * weighted - values * (scale * scale * scale * inner)
    grad_gain = jnp.sum(grad * values * scale, axis=0, keepdims=True)
    return grad_values, grad_gain


def head_masks(rows):
    lane = lax.broadcasted_iota(jnp.int32, (rows, PAIR), 1)
    left = (lane < PAIR // 2).astype(F32)
    return left.astype(BF16), (1.0 - left).astype(BF16)


def attend(queries, keys, values, allowed, bias_of, probs_ref, out_ref):
    q_left, q_right = head_masks(queries.shape[0])
    k_left, k_right = head_masks(keys.shape[0])
    rows = queries.shape[0]
    for pair in range(HEADS // 2):
        lanes = slice(pair * PAIR, (pair + 1) * PAIR)
        query, key, value = queries[:, lanes], keys[:, lanes], values[:, lanes]
        scores = mm_nt(jnp.concatenate([query * q_left, query * q_right], axis=0), key)
        probs = []
        for side in range(2):
            part = scores[side * rows : (side + 1) * rows]
            if bias_of is not None:
                part = part + bias_of(2 * pair + side)
            part = jnp.where(allowed, part, NEG)
            raised = jnp.exp(part - jnp.max(part, axis=-1, keepdims=True))
            weights = raised / jnp.sum(raised, axis=-1, keepdims=True)
            probs_ref[2 * pair + side] = weights
            probs.append(weights.astype(BF16))
        both = jnp.concatenate([value * k_left, value * k_right], axis=0)
        out_ref[:, lanes] = mm(jnp.concatenate(probs, axis=1), both).astype(BF16)


def attend_back(queries, keys, values, grad_out, probs_ref, dq_ref, dk_ref, dv_ref, collect):
    q_left, q_right = head_masks(queries.shape[0])
    k_left, k_right = head_masks(keys.shape[0])
    rows = queries.shape[0]
    for pair in range(HEADS // 2):
        lanes = slice(pair * PAIR, (pair + 1) * PAIR)
        query, key, value, grad = queries[:, lanes], keys[:, lanes], values[:, lanes], grad_out[:, lanes]
        grad_two = jnp.concatenate([grad * q_left, grad * q_right], axis=0)
        query_two = jnp.concatenate([query * q_left, query * q_right], axis=0)
        key_two = jnp.concatenate([key * k_left, key * k_right], axis=0)
        grad_probs = mm_nt(grad_two, value)
        probs, scores = [], []
        for side in range(2):
            weights = probs_ref[2 * pair + side]
            part = grad_probs[side * rows : (side + 1) * rows]
            inner = jnp.sum(weights * part, axis=-1, keepdims=True)
            score = (weights * (part - inner)).astype(BF16)
            if collect is not None:
                collect(2 * pair + side, score)
            probs.append(weights.astype(BF16))
            scores.append(score)
        dq_ref[:, lanes] = mm(jnp.concatenate(scores, axis=1), key_two).astype(BF16)
        dk_ref[:, lanes] = mm_tn(jnp.concatenate(scores, axis=0), query_two).astype(BF16)
        dv_ref[:, lanes] = mm_tn(jnp.concatenate(probs, axis=0), grad_two).astype(BF16)


def load_weights(info, mine, theirs, weights, sems):
    rows = weights.shape[2]
    copies = []
    for source, base in ((mine, 2 * info[0]), (theirs, 2 * (1 - info[0]))):
        for index in range(2):
            copy = pltpu.make_async_copy(
                source.at[:, pl.ds(index * rows, rows), :],
                weights.at[base + index],
                sems.at[len(copies)],
            )
            copy.start()
            copies.append(copy)
    return copies


def whole(weights, index):
    return weights[index].reshape(-1, weights.shape[-1])


def collect_kernel(high, info, *refs):
    pieces, out, sems = refs[:-2], refs[-2], refs[-1]
    copies = []
    for step in range(high):
        owner = lax.rem(info[1] + step, high) * 2
        for other, place in ((0, owner + info[2]), (1, owner + 1 - info[2])):
            copy = pltpu.make_async_copy(
                pieces[2 * step + other], out.at[place], sems.at[2 * step + other]
            )
            copy.start()
            copies.append(copy)
    for copy in copies:
        copy.wait()


def self_forward(seq_count, info, tokens, gain, line, mine, theirs, q_out, k_out, v_out, probs, attn, hidden, weights, sems):
    copies = load_weights(info, mine, theirs, weights, sems)
    rows = tokens.shape[0]
    values = tokens[...].astype(F32)
    _, normed = rms_parts(values, gain[...])
    bounds = read_bounds(info, seq_count)
    allowed = segments(bounds, (rows, rows), 0) == segments(bounds, (rows, rows), 1)
    allowed = allowed & (
        lax.broadcasted_iota(jnp.int32, (rows, rows), 0) >= lax.broadcasted_iota(jnp.int32, (rows, rows), 1)
    )
    live = (segments(bounds, (rows, 1), 0) < seq_count).astype(F32)

    def bias_of(head):
        wide = jnp.broadcast_to(line[head : head + 1, :], (rows, rows))
        return pltpu.roll(wide, 0, 1, stride=1, stride_axis=0)

    for copy in copies:
        copy.wait()
    q_out[...] = mm(normed, whole(weights, 0)).astype(BF16)
    k_out[...] = mm(normed, whole(weights, 1)).astype(BF16)
    v_out[...] = mm(normed, whole(weights, 2)).astype(BF16)
    attend(q_out[...], k_out[...], v_out[...], allowed, bias_of, probs, attn)
    hidden[...] = values + live * mm(attn[...], whole(weights, 3))


def cross_forward(seq_count, info, hidden_one, gain, gain_next, encoder, mine, theirs, q_out, k_out, v_out, probs, attn, hidden, normed_out, weights, sems):
    copies = load_weights(info, mine, theirs, weights, sems)
    rows, enc_rows = hidden_one.shape[0], encoder.shape[0]
    values = hidden_one[...]
    _, normed = rms_parts(values, gain[...])
    bounds = read_bounds(info, seq_count)
    clipped = jnp.minimum(segments(bounds, (rows, enc_rows), 0), seq_count - 1)
    length = enc_rows // seq_count
    place = lax.broadcasted_iota(jnp.int32, (rows, enc_rows), 1)
    key_segment = jnp.zeros((rows, enc_rows), jnp.int32)
    for index in range(1, seq_count):
        key_segment = key_segment + (place >= index * length).astype(jnp.int32)
    allowed = clipped == key_segment
    live = (segments(bounds, (rows, 1), 0) < seq_count).astype(F32)
    for copy in copies:
        copy.wait()
    q_out[...] = mm(normed, whole(weights, 0)).astype(BF16)
    k_out[...] = mm(encoder[...], whole(weights, 1)).astype(BF16)
    v_out[...] = mm(encoder[...], whole(weights, 2)).astype(BF16)
    attend(q_out[...], k_out[...], v_out[...], allowed, None, probs, attn)
    result = values + live * mm(attn[...], whole(weights, 3))
    hidden[...] = result
    normed_out[...] = rms_parts(result, gain_next[...])[1]


def feed_forward(
    seq_count, info, normed_ref, hidden, cotangent, gain, wide_mine, wide_theirs, down_mine, down_theirs,
    mixed, grad_hidden, grad_gain, g_wide_mine, g_wide_other, g_down_mine, g_down_other, total, back,
):
    step = pl.program_id(0)
    flag = info[0] == 0
    rows, width = hidden.shape
    half = width // 2
    bounds = read_bounds(info, seq_count)
    live = (segments(bounds, (rows, 1), 0) < seq_count).astype(F32)
    normed = normed_ref[...]
    branch = (live * cotangent[...].astype(F32)).astype(BF16)
    left, right = branch[:, :half], branch[:, half:]
    b_mine, b_other = choose(flag, left, right), choose(flag, right, left)

    @pl.when(step == 0)
    def _():
        total[...] = jnp.zeros_like(total)
        back[...] = jnp.zeros_like(back)

    own = wide_mine[...].reshape(width, -1)
    other = wide_theirs[...].reshape(width, -1)
    down_own = down_mine[0]
    down_other = down_theirs[0]
    first, second = mm(normed, own), mm(normed, other)
    gate, up = choose(flag, first, second), choose(flag, second, first)
    inner = jnp.tanh(SQRT_2_PI * (gate + 0.044715 * (gate * gate * gate)))
    cdf = 0.5 * (1.0 + inner)
    gelu = gate * cdf
    act = (gelu * up).astype(BF16)
    total[0] += mm(act, down_own)
    total[1] += mm(act, down_other)
    d_act = mm_nt(b_mine, down_own) + mm_nt(b_other, down_other)
    slope = cdf + 0.5 * gate * (1.0 - inner * inner) * (
        SQRT_2_PI * (1.0 + 3 * 0.044715 * (gate * gate))
    )
    d_gate = (d_act * up * slope).astype(BF16)
    d_up = (d_act * gelu).astype(BF16)
    d_own, d_other = choose(flag, d_gate, d_up), choose(flag, d_up, d_gate)
    back[...] += mm_nt(d_own, own) + mm_nt(d_other, other)
    g_wide_mine[...] = mm_tn(normed, d_own).astype(BF16).reshape(g_wide_mine.shape)
    g_wide_other[...] = mm_tn(normed, d_other).astype(BF16).reshape(g_wide_other.shape)
    g_down_mine[0] = mm_tn(act, b_mine).astype(BF16)
    g_down_other[0] = mm_tn(act, b_other).astype(BF16)

    @pl.when(step == pl.num_programs(0) - 1)
    def _():
        one, two = total[0], total[1]
        outcome = jnp.concatenate([choose(flag, one, two), choose(flag, two, one)], axis=1)
        mixed[...] = (hidden[...] + live * outcome).astype(BF16)
        part, term = rms_back(hidden[...], gain[...], back[...])
        grad_hidden[...] = cotangent[...].astype(F32) + part
        grad_gain[...] = term


def cross_backward(
    seq_count, info, grad_in, hidden_one, gain, encoder, queries, keys, values, probs, attn, mine, theirs,
    grad_out, grad_enc, grad_gain, g_mine, g_other, weights, dq, dk, dv, sems,
):
    copies = load_weights(info, mine, theirs, weights, sems)
    rows = hidden_one.shape[0]
    flag = info[0] == 0
    bounds = read_bounds(info, seq_count)
    live = (segments(bounds, (rows, 1), 0) < seq_count).astype(F32)
    grad = grad_in[...]
    branch = (live * grad).astype(BF16)
    _, normed = rms_parts(hidden_one[...], gain[...])
    for copy in copies:
        copy.wait()
    grad_attn = mm_nt(branch, whole(weights, 3)).astype(BF16)
    attend_back(queries[...], keys[...], values[...], grad_attn, probs, dq, dk, dv, None)
    d_query, d_key, d_value = dq[...], dk[...], dv[...]
    source = encoder[...]
    shape = g_mine.shape[0], g_mine.shape[1] // 2, g_mine.shape[2]
    n = shape[1]
    pairs = ((normed, d_query), (source, d_key)), ((source, d_value), (attn[...], branch))
    for index in range(2):
        low, high = pairs[0][index], pairs[1][index]
        for target, take in ((g_mine, flag), (g_other, jnp.logical_not(flag))):
            term = mm_tn(choose(take, low[0], high[0]), choose(take, low[1], high[1]))
            target[:, index * n : (index + 1) * n, :] = term.astype(BF16).reshape(shape)
    grad_enc[...] = mm_nt(d_key, whole(weights, 1)) + mm_nt(d_value, whole(weights, 2))
    part, term = rms_back(hidden_one[...], gain[...], mm_nt(d_query, whole(weights, 0)))
    grad_out[...] = grad + part
    grad_gain[...] = term


def self_backward(
    seq_count, info, grad_in, tokens, gain, queries, keys, values, probs, attn, mine, theirs,
    grad_out, grad_gain, grad_line, g_mine, g_other, weights, dq, dk, dv, sems,
):
    copies = load_weights(info, mine, theirs, weights, sems)
    rows = tokens.shape[0]
    flag = info[0] == 0
    bounds = read_bounds(info, seq_count)
    live = (segments(bounds, (rows, 1), 0) < seq_count).astype(F32)
    grad = grad_in[...]
    branch = (live * grad).astype(BF16)
    inputs = tokens[...].astype(F32)
    _, normed = rms_parts(inputs, gain[...])
    grad_line[...] = jnp.zeros_like(grad_line)
    place = lax.broadcasted_iota(jnp.int32, (rows, rows), 0)
    flip = (place + lax.broadcasted_iota(jnp.int32, (rows, rows), 1) == rows - 1).astype(F32).astype(BF16)

    def collect(head, score):
        turned = pltpu.roll(mm(flip, score), 1, 1, stride=1, stride_axis=0)
        grad_line[head : head + 1, :] = jnp.sum(turned, axis=0, keepdims=True)

    for copy in copies:
        copy.wait()
    grad_attn = mm_nt(branch, whole(weights, 3)).astype(BF16)
    attend_back(queries[...], keys[...], values[...], grad_attn, probs, dq, dk, dv, collect)
    d_query, d_key, d_value = dq[...], dk[...], dv[...]
    shape = g_mine.shape[0], g_mine.shape[1] // 2, g_mine.shape[2]
    n = shape[1]
    pairs = ((normed, d_query), (normed, d_key)), ((normed, d_value), (attn[...], branch))
    for index in range(2):
        low, high = pairs[0][index], pairs[1][index]
        for target, take in ((g_mine, flag), (g_other, jnp.logical_not(flag))):
            term = mm_tn(choose(take, low[0], high[0]), choose(take, low[1], high[1]))
            target[:, index * n : (index + 1) * n, :] = term.astype(BF16).reshape(shape)
    grad_normed = (
        mm_nt(d_query, whole(weights, 0)) + mm_nt(d_key, whole(weights, 1)) + mm_nt(d_value, whole(weights, 2))
    )
    part, term = rms_back(inputs, gain[...], grad_normed)
    grad_out[...] = grad + part
    grad_gain[...] = term


class Links:
    def __init__(self, fsdp_count, replica_count):
        self.count = fsdp_count
        self.high = fsdp_count // 2
        self.replicas = replica_count
        self.place = lax.axis_index("fsdp")
        self.mine_high = self.place // 2
        self.mine_low = self.place % 2
        self.core = lax.axis_index("replica") % 2

    def swap_replica(self, values, bit):
        pairs = [(i, i ^ bit) for i in range(self.replicas)]
        return lax.ppermute(values, "replica", pairs)

    def swap_low(self, values):
        return lax.ppermute(values, "fsdp", [(i, i ^ 1) for i in range(self.count)])

    def ring(self, values):
        return lax.ppermute(
            values, "fsdp", [(i, (i - 2) % self.count) for i in range(self.count)]
        )

    def gather(self, info, local):
        blocks = [local]
        for _ in range(self.high - 1):
            blocks.append(self.ring(blocks[-1]))
        pieces = []
        for block in blocks:
            pieces += [block, self.swap_low(block)]
        nbytes = 2 * len(pieces) * local.size * 2
        mine = pl.pallas_call(
            functools.partial(collect_kernel, self.high),
            out_shape=jax.ShapeDtypeStruct((self.count,) + local.shape, local.dtype),
            in_specs=[SMEM] + [ANY] * len(pieces),
            out_specs=ANY,
            scratch_shapes=[pltpu.SemaphoreType.DMA((len(pieces),))],
            compiler_params=params(16),
            cost_estimate=cost(0, nbytes),
        )(info, *pieces)
        return mine, self.swap_replica(mine, 1)

    def reduce(self, mine, other):
        def add(left, right):
            return (left.astype(F32) + right.astype(F32)).astype(BF16)

        def pick(values, index, axis):
            return lax.dynamic_index_in_dim(values, index, axis, keepdims=False)

        def split(values):
            return values.reshape((self.high, 2) + values.shape[1:])

        mine, got = split(mine), split(self.swap_replica(other, 1))
        away, home = 1 - self.mine_low, self.mine_low
        sent = self.swap_low(add(pick(mine, away, 1), pick(got, away, 1)))
        total = add(add(pick(mine, home, 1), pick(got, home, 1)), sent)

        def block(step):
            return pick(total, (self.mine_high + step) % self.high, 0)

        moving = block(1 % self.high)
        for step in range(2, self.high + 1):
            moving = add(self.ring(moving), block(step % self.high))
        bit = 2
        while bit < self.replicas:
            moving = add(moving, self.swap_replica(moving, bit))
            bit *= 2
        return moving, self.swap_replica(moving, 1)

    def total(self, values):
        bit = 1
        while bit < self.replicas:
            values = values + self.swap_replica(values, bit)
            bit *= 2
        bit = 1
        while bit < self.count:
            pairs = [(i, i ^ bit) for i in range(self.count)]
            values = values + lax.ppermute(values, "fsdp", pairs)
            bit *= 2
        return values


def per_device(
    sizes,
    tokens,
    encoded,
    lengths,
    cotangent,
    norm_self,
    q_self,
    k_self,
    v_self,
    o_self,
    bias_table,
    norm_cross,
    q_cross,
    k_cross,
    v_cross,
    o_cross,
    norm_ff,
    wi_gate,
    wi_up,
    wo_ff,
):
    count, replica_count = sizes
    comm = Links(count, replica_count)
    core_zero = comm.core == 0
    row_count, width = tokens.shape[1:]
    seq_count = lengths.shape[1]
    encoder = encoded[0].reshape(-1, width)
    enc_rows = encoder.shape[0]
    rows = q_self.shape[0]
    hidden_units = wi_gate.shape[1]
    down_rows = wo_ff.shape[0]
    half = width // 2
    info = jnp.concatenate(
        [jnp.stack([comm.core, comm.mine_high, comm.mine_low, comm.place]), lengths[0]]
    ).astype(jnp.int32)
    small = jnp.concatenate([norm_self, norm_cross, norm_ff, bias_table.reshape(-1)])
    small_count = small.shape[0]
    small = jnp.pad(small[None], ((0, 15), (0, width - small_count)))

    first_mine, first_theirs = comm.gather(
        info,
        jnp.concatenate(
            [jnp.where(core_zero, q_self, v_self), jnp.where(core_zero, k_self, o_self), small]
        ),
    )
    second_mine, second_theirs = comm.gather(
        info,
        jnp.concatenate(
            [jnp.where(core_zero, q_cross, v_cross), jnp.where(core_zero, k_cross, o_cross)]
        ),
    )
    wide_mine, wide_theirs = comm.gather(info, jnp.where(core_zero, wi_gate, wi_up))
    down_mine, down_theirs = comm.gather(
        info, jnp.where(core_zero, wo_ff[:, :half], wo_ff[:, half:])
    )

    vectors = first_mine[:, 2 * rows, :small_count].astype(F32)
    gain_one = vectors[:, :rows].reshape(1, -1)
    gain_two = vectors[:, rows : 2 * rows].reshape(1, -1)
    gain_three = vectors[:, 2 * rows : 3 * rows].reshape(1, -1)
    table = vectors[:, 3 * rows :].reshape(-1, HEADS)
    turned = jnp.asarray((-np.arange(row_count)) % row_count, jnp.int32)
    bucket_hot = (
        bucket_of(turned)[:, None] == lax.iota(jnp.int32, table.shape[0])[None, :]
    ).astype(F32)
    line = jnp.dot(bucket_hot, table, precision=lax.Precision.HIGHEST).T
    line = jnp.pad(line, ((0, 16 - HEADS), (0, 0)))

    def shape(*dims, dtype=BF16):
        return jax.ShapeDtypeStruct(dims, dtype)

    act = shape(row_count, width)
    act_enc = shape(enc_rows, width)
    act32 = shape(row_count, width, dtype=F32)
    vec32 = shape(1, width, dtype=F32)
    weight_scratch = pltpu.VMEM((4, count, rows, width), BF16)
    sems = pltpu.SemaphoreType.DMA((4,))
    weight_bytes = 4 * count * rows * width * 2
    pair_flops = 2 * row_count * width * width
    attn_scratch = pltpu.VMEM((row_count, width), BF16)
    enc_scratch = pltpu.VMEM((enc_rows, width), BF16)

    tokens_here = tokens[0]
    queries, keys, values, probs, attn_one, hidden_one = pl.pallas_call(
        functools.partial(self_forward, seq_count),
        out_shape=(act, act, act, shape(HEADS, row_count, row_count, dtype=F32), act, act32),
        in_specs=[SMEM, VMEM, VMEM, VMEM, ANY, ANY],
        out_specs=[VMEM] * 6,
        scratch_shapes=[weight_scratch, sems],
        compiler_params=params(),
        cost_estimate=cost(5 * pair_flops, weight_bytes),
    )(info, tokens_here, gain_one, line, first_mine, first_theirs)

    queries_c, keys_c, values_c, probs_c, attn_two, hidden_two, normed_three = pl.pallas_call(
        functools.partial(cross_forward, seq_count),
        out_shape=(act, act_enc, act_enc, shape(HEADS, row_count, enc_rows, dtype=F32), act, act32, act),
        in_specs=[SMEM, VMEM, VMEM, VMEM, VMEM, ANY, ANY],
        out_specs=[VMEM] * 7,
        scratch_shapes=[weight_scratch, sems],
        compiler_params=params(),
        cost_estimate=cost(5 * pair_flops, weight_bytes),
    )(info, hidden_one, gain_two, gain_three, encoder, second_mine, second_theirs)

    chunk = hidden_units // count

    def fixed(*dims):
        return pl.BlockSpec(dims, lambda j: (0,) * len(dims))

    wide_spec = pl.BlockSpec((count, rows, chunk), lambda j: (0, 0, j))
    down_spec = pl.BlockSpec((1, down_rows, half), lambda j: (j, 0, 0))
    act_spec = fixed(row_count, width)
    mixed, grad_hidden_two, grad_norm_three, g_wide, g_wide_other, g_down, g_down_other = pl.pallas_call(
        functools.partial(feed_forward, seq_count),
        grid=(count,),
        out_shape=(
            act, act32, vec32,
            shape(count, rows, hidden_units), shape(count, rows, hidden_units),
            shape(count, down_rows, half), shape(count, down_rows, half),
        ),
        in_specs=[SMEM, act_spec, act_spec, act_spec, fixed(1, width), wide_spec, wide_spec, down_spec, down_spec],
        out_specs=[act_spec, act_spec, fixed(1, width), wide_spec, wide_spec, down_spec, down_spec],
        scratch_shapes=[pltpu.VMEM((2, row_count, half), F32), pltpu.VMEM((row_count, width), F32)],
        compiler_params=params(),
        cost_estimate=cost(18 * row_count * width * hidden_units, 12 * width * hidden_units),
    )(info, normed_three, hidden_two, cotangent[0], gain_three, wide_mine, wide_theirs, down_mine, down_theirs)
    wide_sum = comm.reduce(g_wide, g_wide_other)
    down_sum = comm.reduce(g_down, g_down_other)

    grads = shape(count, 2 * rows, width)
    grad_hidden_one, grad_encoder, grad_norm_two, g_second, g_second_other = pl.pallas_call(
        functools.partial(cross_backward, seq_count),
        out_shape=(act32, shape(enc_rows, width, dtype=F32), vec32, grads, grads),
        in_specs=[SMEM] + [VMEM] * 9 + [ANY, ANY],
        out_specs=[VMEM] * 5,
        scratch_shapes=[weight_scratch, attn_scratch, enc_scratch, enc_scratch, sems],
        compiler_params=params(),
        cost_estimate=cost(10 * pair_flops, 2 * weight_bytes),
    )(
        info, grad_hidden_two, hidden_one, gain_two, encoder, queries_c, keys_c, values_c, probs_c, attn_two,
        second_mine, second_theirs,
    )
    second_sum = comm.reduce(g_second, g_second_other)

    grad_inputs, grad_norm_one, grad_line, g_first, g_first_other = pl.pallas_call(
        functools.partial(self_backward, seq_count),
        out_shape=(act32, vec32, shape(16, row_count, dtype=F32), grads, grads),
        in_specs=[SMEM] + [VMEM] * 8 + [ANY, ANY],
        out_specs=[VMEM] * 5,
        scratch_shapes=[weight_scratch, attn_scratch, attn_scratch, attn_scratch, sems],
        compiler_params=params(),
        cost_estimate=cost(10 * pair_flops, 2 * weight_bytes),
    )(
        info, grad_hidden_one, tokens_here, gain_one, queries, keys, values, probs, attn_one,
        first_mine, first_theirs,
    )
    first_sum = comm.reduce(g_first, g_first_other)

    grad_table = jnp.dot(grad_line[:HEADS], bucket_hot, precision=lax.Precision.HIGHEST).T
    table_row = jnp.pad(grad_table.reshape(1, -1), ((0, 0), (0, width - grad_table.size)))
    vectors = comm.total(
        jnp.concatenate([grad_norm_one, grad_norm_two, grad_norm_three, table_row])
    )
    owned = lax.dynamic_slice(vectors, (0, comm.place * rows), (3, rows))
    table_size = bias_table.size
    owned_table = lax.dynamic_slice(vectors[3], (comm.place * table_size,), (table_size,))

    def four(pair):
        here, there = (v.astype(F32) for v in pair)
        low, high = jnp.where(core_zero, here, there), jnp.where(core_zero, there, here)
        return low[:rows], low[rows:], high[:rows], high[rows:]

    first, second = four(first_sum), four(second_sum)
    wide_here, wide_there = (v.astype(F32) for v in wide_sum)
    down_here, down_there = (v.astype(F32) for v in down_sum)
    grad_down = jnp.concatenate(
        [jnp.where(core_zero, down_here, down_there), jnp.where(core_zero, down_there, down_here)], axis=1
    )
    return (
        mixed[None],
        grad_inputs[None],
        grad_encoder.reshape(encoded.shape),
        owned[0],
        first[0],
        first[1],
        first[2],
        first[3],
        owned_table.reshape(bias_table.shape),
        owned[1],
        second[0],
        second[1],
        second[2],
        second[3],
        owned[2],
        jnp.where(core_zero, wide_here, wide_there),
        jnp.where(core_zero, wide_there, wide_here),
        grad_down,
    )


def solution(mesh):
    slots = P(("replica", "fsdp"), None, None)
    slots_four = P(("replica", "fsdp"), None, None, None)
    vector, matrix = P("fsdp"), P("fsdp", None)
    weights = (
        (vector,) + (matrix,) * 5 + (vector,) + (matrix,) * 4 + (vector,) + (matrix,) * 3
    )
    return jax.shard_map(
        functools.partial(per_device, (mesh.shape["fsdp"], mesh.shape["replica"])),
        mesh=mesh,
        in_specs=(slots, slots_four, P(("replica", "fsdp"), None), slots) + weights,
        out_specs=(slots, slots, slots_four) + weights,
        check_vma=False,
    )
```

```python
import functools
import math

import jax
import jax.numpy as jnp
import numpy as np
from jax import lax
from jax.experimental import pallas as pl
from jax.experimental.pallas import tpu as pltpu
from jax.sharding import PartitionSpec as P

HEADS = 12
PAIR = 128
EPS = 1e-06
NEG = -1e30
SQRT_2_PI = math.sqrt(2 / math.pi)
bucket_edges = np.array([math.ceil(16 * 8 ** (k / 16)) for k in range(1, 16)], np.int32)

F32 = jnp.float32
BF16 = jnp.bfloat16
VMEM = pl.BlockSpec(memory_space=pltpu.VMEM)
SMEM = pl.BlockSpec(memory_space=pltpu.SMEM)
ANY = pl.BlockSpec(memory_space=pl.ANY)


def params(limit=56):
    return pltpu.CompilerParams(vmem_limit_bytes=limit * 1024 * 1024)


def cost(flops, nbytes):
    return pl.CostEstimate(flops=flops, bytes_accessed=nbytes, transcendentals=0)


def bucket_of(offset):
    distance = jnp.maximum(offset, 0)
    counted = jnp.sum((distance[..., None] >= jnp.asarray(bucket_edges)).astype(jnp.int32), axis=-1)
    return jnp.where(distance < 16, distance, 16 + counted)


def mm(left, right):
    return jnp.dot(left, right, preferred_element_type=F32)


def mm_nt(left, right):
    return lax.dot_general(left, right, (((1,), (1,)), ((), ())), preferred_element_type=F32)


def mm_tn(left, right):
    return lax.dot_general(left, right, (((0,), (0,)), ((), ())), preferred_element_type=F32)


def choose(flag, left, right):
    return lax.select(flag, left, right)


def segments(bounds, shape, axis):
    place = lax.broadcasted_iota(jnp.int32, shape, axis)
    segment = jnp.zeros(shape, jnp.int32)
    for bound in bounds:
        segment = segment + (place >= bound).astype(jnp.int32)
    return segment


def read_bounds(info, seq_count):
    bounds, total = [], 0
    for index in range(seq_count):
        total = total + info[4 + index]
        bounds.append(total)
    return bounds


def rms_parts(values, gain):
    scale = lax.rsqrt(jnp.mean(values * values, axis=-1, keepdims=True) + EPS)
    return scale, (values * scale * gain).astype(BF16)


def rms_back(values, gain, grad):
    scale = lax.rsqrt(jnp.mean(values * values, axis=-1, keepdims=True) + EPS)
    weighted = grad * gain
    inner = jnp.mean(weighted * values, axis=-1, keepdims=True)
    grad_values = scale * weighted - values * (scale * scale * scale * inner)
    grad_gain = jnp.sum(grad * values * scale, axis=0, keepdims=True)
    return grad_values, grad_gain


def head_masks(rows):
    lane = lax.broadcasted_iota(jnp.int32, (rows, PAIR), 1)
    left = (lane < PAIR // 2).astype(F32)
    return left.astype(BF16), (1.0 - left).astype(BF16)


def attend(queries, keys, values, allowed, bias_of, probs_ref, out_ref):
    q_left, q_right = head_masks(queries.shape[0])
    k_left, k_right = head_masks(keys.shape[0])
    rows = queries.shape[0]
    for pair in range(HEADS // 2):
        lanes = slice(pair * PAIR, (pair + 1) * PAIR)
        query, key, value = queries[:, lanes], keys[:, lanes], values[:, lanes]
        scores = mm_nt(jnp.concatenate([query * q_left, query * q_right], axis=0), key)
        probs = []
        for side in range(2):
            part = scores[side * rows : (side + 1) * rows]
            if bias_of is not None:
                part = part + bias_of(2 * pair + side)
            part = jnp.where(allowed, part, NEG)
            raised = jnp.exp(part - jnp.max(part, axis=-1, keepdims=True))
            weights = raised / jnp.sum(raised, axis=-1, keepdims=True)
            probs_ref[2 * pair + side] = weights
            probs.append(weights.astype(BF16))
        both = jnp.concatenate([value * k_left, value * k_right], axis=0)
        out_ref[:, lanes] = mm(jnp.concatenate(probs, axis=1), both).astype(BF16)


def attend_back(queries, keys, values, grad_out, probs_ref, dq_ref, dk_ref, dv_ref, collect):
    q_left, q_right = head_masks(queries.shape[0])
    k_left, k_right = head_masks(keys.shape[0])
    rows = queries.shape[0]
    for pair in range(HEADS // 2):
        lanes = slice(pair * PAIR, (pair + 1) * PAIR)
        query, key, value, grad = queries[:, lanes], keys[:, lanes], values[:, lanes], grad_out[:, lanes]
        grad_two = jnp.concatenate([grad * q_left, grad * q_right], axis=0)
        query_two = jnp.concatenate([query * q_left, query * q_right], axis=0)
        key_two = jnp.concatenate([key * k_left, key * k_right], axis=0)
        grad_probs = mm_nt(grad_two, value)
        probs, scores = [], []
        for side in range(2):
            weights = probs_ref[2 * pair + side]
            part = grad_probs[side * rows : (side + 1) * rows]
            inner = jnp.sum(weights * part, axis=-1, keepdims=True)
            score = (weights * (part - inner)).astype(BF16)
            if collect is not None:
                collect(2 * pair + side, score)
            probs.append(weights.astype(BF16))
            scores.append(score)
        dq_ref[:, lanes] = mm(jnp.concatenate(scores, axis=1), key_two).astype(BF16)
        dk_ref[:, lanes] = mm_tn(jnp.concatenate(scores, axis=0), query_two).astype(BF16)
        dv_ref[:, lanes] = mm_tn(jnp.concatenate(probs, axis=0), grad_two).astype(BF16)


def owners_of(info):
    core, side = info[0], info[3]
    return 2 * core + side, 2 * core + 1 - side, 2 * (1 - core) + side, 2 * (1 - core) + 1 - side


def load_weights(info, mine, theirs, weights, sems):
    rows = weights.shape[2]
    copies = []
    for source, base in ((mine, 2 * info[0]), (theirs, 2 * (1 - info[0]))):
        for index in range(2):
            copy = pltpu.make_async_copy(
                source.at[:, pl.ds(index * rows, rows), :],
                weights.at[base + index],
                sems.at[len(copies)],
            )
            copy.start()
            copies.append(copy)
    return copies


def weight_grads(info, lefts, grads, targets):
    for target, place in zip(targets, owners_of(info)):
        left = lefts[place] if hasattr(lefts, "at") else choose(place == 3, lefts[1], lefts[0])
        target[...] = mm_tn(left, grads[place]).astype(BF16).reshape(target.shape)


def whole(weights, index):
    return weights[index].reshape(-1, weights.shape[-1])


def collect_kernel(high, info, *refs):
    pieces, out, sems = refs[:-2], refs[-2], refs[-1]
    copies = []
    for step in range(high):
        owner = lax.bitwise_xor(info[1], step) * 2
        for other, place in ((0, owner + info[2]), (1, owner + 1 - info[2])):
            copy = pltpu.make_async_copy(
                pieces[2 * step + other], out.at[place], sems.at[2 * step + other]
            )
            copy.start()
            copies.append(copy)
    for copy in copies:
        copy.wait()


def self_forward(seq_count, info, tokens, gain, line, mine, theirs, q_out, k_out, v_out, probs, attn, hidden, weights, sems):
    copies = load_weights(info, mine, theirs, weights, sems)
    rows = tokens.shape[0]
    values = tokens[...].astype(F32)
    _, normed = rms_parts(values, gain[...])
    bounds = read_bounds(info, seq_count)
    allowed = segments(bounds, (rows, rows), 0) == segments(bounds, (rows, rows), 1)
    allowed = allowed & (
        lax.broadcasted_iota(jnp.int32, (rows, rows), 0) >= lax.broadcasted_iota(jnp.int32, (rows, rows), 1)
    )
    live = (segments(bounds, (rows, 1), 0) < seq_count).astype(F32)

    def bias_of(head):
        wide = jnp.broadcast_to(line[head : head + 1, :], (rows, rows))
        return pltpu.roll(wide, 0, 1, stride=1, stride_axis=0)

    for copy in copies:
        copy.wait()
    q_out[...] = mm(normed, whole(weights, 0)).astype(BF16)
    k_out[...] = mm(normed, whole(weights, 1)).astype(BF16)
    v_out[...] = mm(normed, whole(weights, 2)).astype(BF16)
    attend(q_out[...], k_out[...], v_out[...], allowed, bias_of, probs, attn)
    hidden[...] = values + live * mm(attn[...], whole(weights, 3))


def cross_forward(seq_count, info, hidden_one, gain, gain_next, encoder, mine, theirs, q_out, k_out, v_out, probs, attn, hidden, normed_out, weights, sems):
    copies = load_weights(info, mine, theirs, weights, sems)
    rows, enc_rows = hidden_one.shape[0], encoder.shape[0]
    values = hidden_one[...]
    _, normed = rms_parts(values, gain[...])
    bounds = read_bounds(info, seq_count)
    clipped = jnp.minimum(segments(bounds, (rows, enc_rows), 0), seq_count - 1)
    length = enc_rows // seq_count
    place = lax.broadcasted_iota(jnp.int32, (rows, enc_rows), 1)
    key_segment = jnp.zeros((rows, enc_rows), jnp.int32)
    for index in range(1, seq_count):
        key_segment = key_segment + (place >= index * length).astype(jnp.int32)
    allowed = clipped == key_segment
    live = (segments(bounds, (rows, 1), 0) < seq_count).astype(F32)
    for copy in copies:
        copy.wait()
    q_out[...] = mm(normed, whole(weights, 0)).astype(BF16)
    k_out[...] = mm(encoder[...], whole(weights, 1)).astype(BF16)
    v_out[...] = mm(encoder[...], whole(weights, 2)).astype(BF16)
    attend(q_out[...], k_out[...], v_out[...], allowed, None, probs, attn)
    result = values + live * mm(attn[...], whole(weights, 3))
    hidden[...] = result
    normed_out[...] = rms_parts(result, gain_next[...])[1]


def unpack_down(packed, owner, wide):
    sub = packed.shape[1] // 3
    return jnp.concatenate(
        [
            jnp.concatenate(
                [packed[owner, sub * g : sub * (g + 1), wide + PAIR * i : wide + PAIR * (i + 1)] for g in range(3)],
                axis=1,
            )
            for i in range(4)
        ],
        axis=0,
    )


def pack_down(target, owner, wide, values):
    sub = target.shape[1] // 3
    for i in range(4):
        for g in range(3):
            target[owner, sub * g : sub * (g + 1), wide + PAIR * i : wide + PAIR * (i + 1)] = values[
                sub * i : sub * (i + 1), PAIR * g : PAIR * (g + 1)
            ]


def feed_forward(last, seq_count, info, normed_ref, cotangent, mine, theirs, *refs):
    if last:
        hidden, gain, total, back, mixed, grad_hidden, grad_gain, g_mine, g_other = refs
    else:
        total_out, back_out, g_mine, g_other = refs
    flag = info[0] == 0
    rows, width = cotangent.shape
    half = width // 2
    count, _, packed = mine.shape
    wide = packed * 2 // 3
    units = wide // count
    owners = max(1, 256 // units)
    chunk = owners * units
    bounds = read_bounds(info, seq_count)
    live = (segments(bounds, (rows, 1), 0) < seq_count).astype(F32)
    normed = normed_ref[...]
    branch = (live * cotangent[...].astype(F32)).astype(BF16)
    left, right = branch[:, :half], branch[:, half:]
    b_mine, b_other = choose(flag, left, right), choose(flag, right, left)
    if last:
        sum_mine, sum_other, sum_back = total[0], total[1], back[...]
    else:
        sum_mine = jnp.zeros((rows, half), F32)
        sum_other = jnp.zeros((rows, half), F32)
        sum_back = jnp.zeros((rows, width), F32)
    for step in range(wide // chunk):
        lanes = slice(step * chunk, (step + 1) * chunk)
        places = range(step * owners, (step + 1) * owners)
        own = mine[:, :, lanes].reshape(width, chunk)
        other = theirs[:, :, lanes].reshape(width, chunk)
        down_own = jnp.concatenate([unpack_down(mine, o, wide) for o in places], axis=0)
        down_other = jnp.concatenate([unpack_down(theirs, o, wide) for o in places], axis=0)
        first, second = mm(normed, own), mm(normed, other)
        gate, up = choose(flag, first, second), choose(flag, second, first)
        inner = jnp.tanh(SQRT_2_PI * (gate + 0.044715 * (gate * gate * gate)))
        cdf = 0.5 * (1.0 + inner)
        gelu = gate * cdf
        act = (gelu * up).astype(BF16)
        sum_mine += mm(act, down_own)
        sum_other += mm(act, down_other)
        d_act = mm_nt(b_mine, down_own) + mm_nt(b_other, down_other)
        slope = cdf + 0.5 * gate * (1.0 - inner * inner) * (
            SQRT_2_PI * (1.0 + 3 * 0.044715 * (gate * gate))
        )
        d_gate = (d_act * up * slope).astype(BF16)
        d_up = (d_act * gelu).astype(BF16)
        d_own, d_other = choose(flag, d_gate, d_up), choose(flag, d_up, d_gate)
        sum_back += mm_nt(d_own, own) + mm_nt(d_other, other)
        g_mine[:, :, lanes] = mm_tn(normed, d_own).astype(BF16).reshape(count, -1, chunk)
        g_other[:, :, lanes] = mm_tn(normed, d_other).astype(BF16).reshape(count, -1, chunk)
        down_grad = mm_tn(act, b_mine).astype(BF16)
        down_grad_other = mm_tn(act, b_other).astype(BF16)
        for index, owner in enumerate(places):
            here = slice(index * units, (index + 1) * units)
            pack_down(g_mine, owner, wide, down_grad[here])
            pack_down(g_other, owner, wide, down_grad_other[here])
    if last:
        outcome = jnp.concatenate(
            [choose(flag, sum_mine, sum_other), choose(flag, sum_other, sum_mine)], axis=1
        )
        mixed[...] = (hidden[...] + live * outcome).astype(BF16)
        part, term = rms_back(hidden[...], gain[...], sum_back)
        grad_hidden[...] = cotangent[...].astype(F32) + part
        grad_gain[...] = term
    else:
        total_out[0] = sum_mine
        total_out[1] = sum_other
        back_out[...] = sum_back


def cross_backward(
    seq_count, info, grad_in, hidden_one, gain, encoder, queries, keys, values, probs, attn, mine, theirs,
    grad_out, grad_enc, grad_gain, g_own, g_side, g_core, g_far, weights, grads, lefts, sems,
):
    copies = load_weights(info, mine, theirs, weights, sems)
    rows = hidden_one.shape[0]
    bounds = read_bounds(info, seq_count)
    live = (segments(bounds, (rows, 1), 0) < seq_count).astype(F32)
    grad = grad_in[...]
    branch = (live * grad).astype(BF16)
    _, normed = rms_parts(hidden_one[...], gain[...])
    lefts[0] = normed
    lefts[1] = encoder[...]
    lefts[2] = encoder[...]
    lefts[3] = attn[...]
    grads[3] = branch
    for copy in copies:
        copy.wait()
    grad_attn = mm_nt(branch, whole(weights, 3)).astype(BF16)
    attend_back(queries[...], keys[...], values[...], grad_attn, probs, grads.at[0], grads.at[1], grads.at[2], None)
    weight_grads(info, lefts, grads, (g_own, g_side, g_core, g_far))
    d_query, d_key, d_value = grads[0], grads[1], grads[2]
    grad_enc[...] = mm_nt(d_key, whole(weights, 1)) + mm_nt(d_value, whole(weights, 2))
    part, term = rms_back(hidden_one[...], gain[...], mm_nt(d_query, whole(weights, 0)))
    grad_out[...] = grad + part
    grad_gain[...] = term


def self_backward(
    seq_count, info, grad_in, tokens, gain, queries, keys, values, probs, attn, mine, theirs,
    grad_out, grad_gain, grad_line, g_own, g_side, g_core, g_far, weights, grads, sems,
):
    copies = load_weights(info, mine, theirs, weights, sems)
    rows = tokens.shape[0]
    bounds = read_bounds(info, seq_count)
    live = (segments(bounds, (rows, 1), 0) < seq_count).astype(F32)
    grad = grad_in[...]
    branch = (live * grad).astype(BF16)
    inputs = tokens[...].astype(F32)
    _, normed = rms_parts(inputs, gain[...])
    grad_line[...] = jnp.zeros_like(grad_line)
    grads[3] = branch
    place = lax.broadcasted_iota(jnp.int32, (rows, rows), 0)
    flip = (place + lax.broadcasted_iota(jnp.int32, (rows, rows), 1) == rows - 1).astype(F32).astype(BF16)

    def collect(head, score):
        turned = pltpu.roll(mm(flip, score), 1, 1, stride=1, stride_axis=0)
        grad_line[head : head + 1, :] = jnp.sum(turned, axis=0, keepdims=True)

    for copy in copies:
        copy.wait()
    grad_attn = mm_nt(branch, whole(weights, 3)).astype(BF16)
    attend_back(
        queries[...], keys[...], values[...], grad_attn, probs, grads.at[0], grads.at[1], grads.at[2], collect
    )
    weight_grads(info, (normed, attn[...]), grads, (g_own, g_side, g_core, g_far))
    d_query, d_key, d_value = grads[0], grads[1], grads[2]
    grad_normed = (
        mm_nt(d_query, whole(weights, 0)) + mm_nt(d_key, whole(weights, 1)) + mm_nt(d_value, whole(weights, 2))
    )
    part, term = rms_back(inputs, gain[...], grad_normed)
    grad_out[...] = grad + part
    grad_gain[...] = term


class Links:
    def __init__(self, fsdp_count, replica_count):
        self.count = fsdp_count
        self.high = fsdp_count // 2
        self.replicas = replica_count
        self.place = lax.axis_index("fsdp")
        self.mine_high = self.place // 2
        self.mine_low = self.place % 2
        self.core = lax.axis_index("replica") % 2
        self.side = lax.axis_index("replica") // 2 % 2

    def swap_replica(self, values, bit):
        pairs = [(i, i ^ bit) for i in range(self.replicas)]
        return lax.ppermute(values, "replica", pairs)

    def swap_low(self, values):
        return lax.ppermute(values, "fsdp", [(i, i ^ 1) for i in range(self.count)])

    def swap_high(self, values, step):
        return lax.ppermute(values, "fsdp", [(i, i ^ (2 * step)) for i in range(self.count)])

    def collect(self, info, pieces):
        local = pieces[0]
        nbytes = 2 * len(pieces) * local.size * 2
        return pl.pallas_call(
            functools.partial(collect_kernel, self.high),
            out_shape=jax.ShapeDtypeStruct((self.count,) + local.shape, local.dtype),
            in_specs=[SMEM] + [ANY] * len(pieces),
            out_specs=ANY,
            scratch_shapes=[pltpu.SemaphoreType.DMA((len(pieces),))],
            compiler_params=params(16),
            cost_estimate=cost(0, nbytes),
        )(info, *pieces)

    def gather(self, locals_, window):
        got, sent, order = {}, [], []
        for index, local in enumerate(locals_):
            got[index, 0, 0] = local
            ring = []
            bit = self.high // 2
            keys = [0]
            while bit:
                for key in list(keys):
                    keys.append(key | bit)
                    ring.append(((index, key, 0), (index, key | bit, 0), bit))
                bit //= 2
            side = [((index, key, 0), (index, key, 1), 0) for key in keys]
            order.append((ring, side))
        queue, pending = [], []
        for ring, side in order:
            side = list(side)
            for item in ring:
                queue.append(item)
                if pending:
                    queue.append(pending.pop(0))
                elif side:
                    queue.append(side.pop(0))
            pending += side
        queue += pending
        ready = set((i, 0, 0) for i in range(len(locals_)))
        waiting = list(queue)
        queue = []
        while waiting:
            place = next(i for i, item in enumerate(waiting) if item[0] in ready)
            item = waiting.pop(place)
            ready.add(item[1])
            queue.append(item)
        for number, (source, target, bit) in enumerate(queue):
            values = got[source]
            if number >= window:
                old = queue[number - window][1]
                if old != source:
                    values, got[old] = lax.optimization_barrier((values, got[old]))
            got[target] = self.swap_high(values, bit) if bit else self.swap_low(values)
        return [
            [got[index, key, side] for key in range(self.high) for side in range(2)]
            for index in range(len(locals_))
        ]

    def split(self, values):
        values = values.reshape((self.high, 2) + values.shape[1:])
        return pick(values, 1 - self.mine_low, 1), pick(values, self.mine_low, 1)


class Sequence:
    def __init__(self, token):
        self.token = token

    def __call__(self, values):
        return after(values, self.token)[0]

    def mark(self, values):
        self.token = values
        return values


class Sums:
    def __init__(self, comm, sequence):
        self.comm, self.sequence = comm, sequence

    def low(self, *parts):
        parts = list(parts)
        parts[0] = self.sequence(parts[0])
        pairs = [self.comm.split(part) for part in parts]
        self.home = [pair[1] for pair in pairs]
        sent = self.sequence.mark(add(*[pair[0] for pair in pairs]))
        self.got = self.comm.swap_low(sent)
        self.bit = 0

    def step(self):
        comm = self.comm
        if not self.bit:
            total = add(self.sequence(self.got), *self.home)
            self.held = {key: pick(total, comm.mine_high ^ key, 0) for key in range(comm.high)}
            self.bit = 1
        else:
            self.receive()
            self.bit *= 2
        if self.bit >= comm.high:
            return False
        self.away = [key for key in self.held if key & self.bit]
        sent = self.sequence.mark(jnp.stack([self.held.pop(key) for key in self.away]))
        self.got = comm.swap_high(sent, self.bit)
        return True

    def receive(self):
        got = self.sequence(self.got)
        for index, key in enumerate(self.away):
            self.held[key ^ self.bit] = add(self.held[key ^ self.bit], got[index])

    def finish(self):
        while self.step():
            pass
        return self.sequence.mark(self.held[0])

    def over_replicas(self, values, bit):
        while bit < self.comm.replicas:
            values = add(values, self.comm.swap_replica(values, bit))
            bit *= 2
        return values


def add(*terms):
    return functools.reduce(jnp.add, [term.astype(F32) for term in terms]).astype(BF16)


def pick(values, index, axis):
    return lax.dynamic_index_in_dim(values, index, axis, keepdims=False)


def after(values, *tokens):
    return lax.optimization_barrier((values,) + tokens)


def per_device(
    sizes,
    tokens,
    encoded,
    lengths,
    cotangent,
    norm_self,
    q_self,
    k_self,
    v_self,
    o_self,
    bias_table,
    norm_cross,
    q_cross,
    k_cross,
    v_cross,
    o_cross,
    norm_ff,
    wi_gate,
    wi_up,
    wo_ff,
):
    count, replica_count = sizes
    comm = Links(count, replica_count)
    core_zero = comm.core == 0
    row_count, width = tokens.shape[1:]
    seq_count = lengths.shape[1]
    encoder = encoded[0].reshape(-1, width)
    enc_rows = encoder.shape[0]
    rows = q_self.shape[0]
    hidden_units = wi_gate.shape[1]
    down_rows = wo_ff.shape[0]
    half = width // 2
    info = jnp.concatenate(
        [jnp.stack([comm.core, comm.mine_high, comm.mine_low, comm.side]), lengths[0]]
    ).astype(jnp.int32)
    small = jnp.concatenate([norm_self, norm_cross, norm_ff, bias_table.reshape(-1)])
    small_count = small.shape[0]
    small = jnp.pad(small[None], ((0, 15), (0, width - small_count)))

    units = down_rows // 2
    side_zero = comm.side == 0
    wide = jnp.where(core_zero, wi_gate, wi_up).reshape(rows, count, 2, units)

    wide = pick(wide, comm.side, 2).reshape(rows, -1)
    down = pick(wo_ff.reshape(2, units, width), comm.side, 0)
    down = jnp.where(core_zero, down[:, :half], down[:, half:])
    down = down.reshape(4, units // 4, 3, PAIR).transpose(2, 1, 0, 3).reshape(rows, -1)
    feed_local = jnp.concatenate([wide, down], axis=1)
    first_local = jnp.concatenate(
        [jnp.where(core_zero, q_self, v_self), jnp.where(core_zero, k_self, o_self), small]
    )
    second_local = jnp.concatenate(
        [jnp.where(core_zero, q_cross, v_cross), jnp.where(core_zero, k_cross, o_cross)]
    )
    feed_pieces, first_pieces, second_pieces = comm.gather(
        [feed_local, first_local, second_local], 4
    )
    feed_one = comm.collect(info, feed_pieces)
    feed_two = comm.swap_replica(feed_one, 2)
    feed_one_theirs = comm.swap_replica(feed_one, 1)
    first_mine = comm.collect(info, first_pieces)
    first_theirs = comm.swap_replica(first_mine, 1)

    vectors = first_mine[:, 2 * rows, :small_count].astype(F32)
    gain_one = vectors[:, :rows].reshape(1, -1)
    gain_two = vectors[:, rows : 2 * rows].reshape(1, -1)
    gain_three = vectors[:, 2 * rows : 3 * rows].reshape(1, -1)
    table = vectors[:, 3 * rows :].reshape(-1, HEADS)
    turned = jnp.asarray((-np.arange(row_count)) % row_count, jnp.int32)
    bucket_hot = (
        bucket_of(turned)[:, None] == lax.iota(jnp.int32, table.shape[0])[None, :]
    ).astype(F32)
    line = jnp.dot(bucket_hot, table, precision=lax.Precision.HIGHEST).T
    line = jnp.pad(line, ((0, 16 - HEADS), (0, 0)))

    def shape(*dims, dtype=BF16):
        return jax.ShapeDtypeStruct(dims, dtype)

    act = shape(row_count, width)
    act_enc = shape(enc_rows, width)
    act32 = shape(row_count, width, dtype=F32)
    vec32 = shape(1, width, dtype=F32)
    weight_scratch = pltpu.VMEM((4, count, rows, width), BF16)
    sems = pltpu.SemaphoreType.DMA((4,))
    weight_bytes = 4 * count * rows * width * 2
    pair_flops = 2 * row_count * width * width
    attn_scratch = pltpu.VMEM((4, row_count, width), BF16)

    tokens_here = tokens[0]
    queries, keys, values, probs, attn_one, hidden_one = pl.pallas_call(
        functools.partial(self_forward, seq_count),
        out_shape=(act, act, act, shape(HEADS, row_count, row_count, dtype=F32), act, act32),
        in_specs=[SMEM, VMEM, VMEM, VMEM] + [ANY] * 2,
        out_specs=[VMEM] * 6,
        scratch_shapes=[weight_scratch, sems],
        compiler_params=params(),
        cost_estimate=cost(5 * pair_flops, weight_bytes),
    )(info, tokens_here, gain_one, line, first_mine, first_theirs)

    second_mine = comm.collect(info, second_pieces)
    second_theirs = comm.swap_replica(second_mine, 1)
    feed_two_theirs = comm.swap_replica(feed_two, 1)
    queries_c, keys_c, values_c, probs_c, attn_two, hidden_two, normed_three = pl.pallas_call(
        functools.partial(cross_forward, seq_count),
        out_shape=(act, act_enc, act_enc, shape(HEADS, row_count, enc_rows, dtype=F32), act, act32, act),
        in_specs=[SMEM, VMEM, VMEM, VMEM, VMEM] + [ANY] * 2,
        out_specs=[VMEM] * 7,
        scratch_shapes=[weight_scratch, sems],
        compiler_params=params(),
        cost_estimate=cost(5 * pair_flops, weight_bytes),
    )(info, hidden_one, gain_two, gain_three, encoder, second_mine, second_theirs)

    packed = shape(*feed_one.shape)
    feed_cost = cost(9 * row_count * width * hidden_units, 12 * width * hidden_units)
    total, back, g_one, g_one_other = pl.pallas_call(
        functools.partial(feed_forward, False, seq_count),
        out_shape=(shape(2, row_count, half, dtype=F32), act32, packed, packed),
        in_specs=[SMEM] + [VMEM] * 4,
        out_specs=[VMEM] * 4,
        compiler_params=params(),
        cost_estimate=feed_cost,
    )(info, normed_three, cotangent[0], feed_one, feed_one_theirs)
    mixed, grad_hidden_two, grad_norm_three, g_two, g_two_other = pl.pallas_call(
        functools.partial(feed_forward, True, seq_count),
        out_shape=(act, act32, vec32, packed, packed),
        in_specs=[SMEM] + [VMEM] * 8,
        out_specs=[VMEM] * 5,
        compiler_params=params(),
        cost_estimate=feed_cost,
    )(info, normed_three, cotangent[0], feed_two, feed_two_theirs, hidden_two, gain_three, total, back)

    sequence = Sequence(grad_norm_three)
    one, two, second, first = (Sums(comm, sequence) for _ in range(4))
    one_got = comm.swap_replica(g_one_other, 1)
    two_got = comm.swap_replica(g_two_other, 1)
    one.low(g_one, one_got)
    grad_hidden_two = sequence(grad_hidden_two)

    grads = shape(count, rows, width)
    grad_hidden_one, grad_encoder, grad_norm_two, *g_second = pl.pallas_call(
        functools.partial(cross_backward, seq_count),
        out_shape=(act32, shape(enc_rows, width, dtype=F32), vec32) + (grads,) * 4,
        in_specs=[SMEM] + [VMEM] * 9 + [ANY] * 2,
        out_specs=[VMEM] * 7,
        scratch_shapes=[weight_scratch, attn_scratch, attn_scratch, sems],
        compiler_params=params(),
        cost_estimate=cost(10 * pair_flops, 2 * weight_bytes),
    )(
        info, grad_hidden_two, hidden_one, gain_two, encoder, queries_c, keys_c, values_c, probs_c, attn_two,
        second_mine, second_theirs,
    )
    def across(g_own, g_side, g_core, g_far):
        from_far = comm.swap_replica(g_far, 1)
        from_core = comm.swap_replica(g_core, 1)

        def finish():
            side = sequence.mark(add(sequence(from_far), g_side))
            return g_own, from_core, comm.swap_replica(side, 2)

        return finish

    sequence.mark(grad_norm_two)
    two.low(g_two, two_got)
    second_parts = across(*g_second)()
    grad_hidden_one = sequence(grad_hidden_one)

    grad_inputs, grad_norm_one, grad_line, *g_first = pl.pallas_call(
        functools.partial(self_backward, seq_count),
        out_shape=(act32, vec32, shape(16, row_count, dtype=F32)) + (grads,) * 4,
        in_specs=[SMEM] + [VMEM] * 8 + [ANY] * 2,
        out_specs=[VMEM] * 7,
        scratch_shapes=[weight_scratch, attn_scratch, sems],
        compiler_params=params(),
        cost_estimate=cost(10 * pair_flops, 2 * weight_bytes),
    )(
        info, grad_hidden_one, tokens_here, gain_one, queries, keys, values, probs, attn_one,
        first_mine, first_theirs,
    )
    sequence.mark(grad_norm_one)
    first_across = across(*g_first)
    one.step()
    second.low(*second_parts)
    first_parts = first_across()
    grad_table = jnp.dot(grad_line[:HEADS], bucket_hot, precision=lax.Precision.HIGHEST).T
    table_row = jnp.pad(grad_table.reshape(1, -1), ((0, 0), (0, width - grad_table.size)))
    vectors = jnp.concatenate([grad_norm_one, grad_norm_two, grad_norm_three, table_row])
    steps = [("replica", 1 << k) for k in range(replica_count.bit_length() - 1)]
    steps += [("fsdp", 1 << k) for k in range(count.bit_length() - 1)]

    def small_step():
        axis, bit = steps.pop(0)
        size = replica_count if axis == "replica" else count
        return lax.ppermute(sequence(vectors), axis, [(i, i ^ bit) for i in range(size)])

    def small_sum(got):
        return vectors + sequence(got)

    got = small_step()
    one.step()
    two.step()
    vectors = small_sum(got)
    got = small_step()
    second.step()
    first.low(*first_parts)
    vectors = small_sum(got)
    got = small_step()
    one_part = one.finish()
    two.step()
    second.step()
    vectors = small_sum(got)
    got = small_step()
    first.step()
    vectors = small_sum(got)
    got = small_step()
    two_part = two.finish()
    one_cross, two_cross = comm.swap_replica(two_part, 2), comm.swap_replica(one_part, 2)
    first.step()
    second_sum = second.over_replicas(second.finish(), 4)
    second_cross, second_core = comm.swap_replica(second_sum, 2), comm.swap_replica(second_sum, 1)
    one_sum = one.over_replicas(add(one_part, sequence(one_cross)), 4)
    two_sum = two.over_replicas(add(two_part, two_cross), 4)
    sequence.mark(two_sum)
    there = comm.swap_replica(one_sum, 1), comm.swap_replica(two_sum, 1)
    vectors = small_sum(got)
    while steps:
        vectors = small_sum(small_step())
    first_sum = first.over_replicas(first.finish(), 4)
    first_cross, first_core = comm.swap_replica(first_sum, 2), comm.swap_replica(first_sum, 1)
    second_far = comm.swap_replica(second_cross, 1)
    first_far = comm.swap_replica(first_cross, 1)

    def four(own, across, core, far):
        zero, one = jnp.where(side_zero, own, across), jnp.where(side_zero, across, own)
        two, three = jnp.where(side_zero, core, far), jnp.where(side_zero, far, core)
        return [
            jnp.where(core_zero, left, right).astype(F32)
            for left, right in ((zero, two), (one, three), (two, zero), (three, one))
        ]

    owned = lax.dynamic_slice(vectors, (0, comm.place * rows), (3, rows))
    table_size = bias_table.size
    owned_table = lax.dynamic_slice(vectors[3], (comm.place * table_size,), (table_size,))

    second = four(second_sum, second_cross, second_core, second_far)
    def by_side(one, two):
        return jnp.where(side_zero, one, two), jnp.where(side_zero, two, one)

    here, there = by_side(one_sum, two_sum), by_side(*there)
    wide_units = hidden_units // 2

    def wide_grad(parts):
        parts = [part[:, :wide_units].reshape(rows, count, 1, units) for part in parts]
        return jnp.concatenate(parts, axis=2).reshape(rows, hidden_units).astype(F32)

    def down_grad(parts):
        parts = [
            part[:, wide_units:].reshape(3, units // 4, 4, PAIR).transpose(2, 1, 0, 3).reshape(units, half)
            for part in parts
        ]
        return jnp.concatenate(parts, axis=0)

    low = [jnp.where(core_zero, one, two) for one, two in zip(here, there)]
    high = [jnp.where(core_zero, two, one) for one, two in zip(here, there)]
    grad_down = jnp.concatenate([down_grad(low), down_grad(high)], axis=1).astype(F32)
    grad_gate, grad_up = wide_grad(low), wide_grad(high)
    first = four(first_sum, first_cross, after(first_core, grad_gate, grad_up, grad_down, *second)[0], first_far)
    return (
        mixed[None],
        grad_inputs[None],
        grad_encoder.reshape(encoded.shape),
        owned[0],
        first[0],
        first[1],
        first[2],
        first[3],
        owned_table.reshape(bias_table.shape),
        owned[1],
        second[0],
        second[1],
        second[2],
        second[3],
        owned[2],
        grad_gate,
        grad_up,
        grad_down,
    )


def solution(mesh):
    slots = P(("replica", "fsdp"), None, None)
    slots_four = P(("replica", "fsdp"), None, None, None)
    vector, matrix = P("fsdp"), P("fsdp", None)
    weights = (
        (vector,) + (matrix,) * 5 + (vector,) + (matrix,) * 4 + (vector,) + (matrix,) * 3
    )
    return jax.shard_map(
        functools.partial(per_device, (mesh.shape["fsdp"], mesh.shape["replica"])),
        mesh=mesh,
        in_specs=(slots, slots_four, P(("replica", "fsdp"), None), slots) + weights,
        out_specs=(slots, slots, slots_four) + weights,
        check_vma=False,
    )
```

```python
import functools
import math

import jax
import jax.numpy as jnp
import numpy as np
from jax import lax
from jax.experimental import pallas as pl
from jax.experimental.pallas import tpu as pltpu
from jax.sharding import PartitionSpec as P

HEADS = 12
PAIR = 128
EPS = 1e-06
NEG = -1e30
SQRT_2_PI = math.sqrt(2 / math.pi)
bucket_edges = np.array([math.ceil(16 * 8 ** (k / 16)) for k in range(1, 16)], np.int32)

F32 = jnp.float32
BF16 = jnp.bfloat16
VMEM = pl.BlockSpec(memory_space=pltpu.VMEM)
SMEM = pl.BlockSpec(memory_space=pltpu.SMEM)
ANY = pl.BlockSpec(memory_space=pl.ANY)


def params(limit=56):
    return pltpu.CompilerParams(vmem_limit_bytes=limit * 1024 * 1024)


def cost(flops, nbytes):
    return pl.CostEstimate(flops=flops, bytes_accessed=nbytes, transcendentals=0)


def bucket_of(offset):
    distance = jnp.maximum(offset, 0)
    counted = jnp.sum((distance[..., None] >= jnp.asarray(bucket_edges)).astype(jnp.int32), axis=-1)
    return jnp.where(distance < 16, distance, 16 + counted)


def mm(left, right):
    return jnp.dot(left, right, preferred_element_type=F32)


def mm_nt(left, right):
    return lax.dot_general(left, right, (((1,), (1,)), ((), ())), preferred_element_type=F32)


def mm_tn(left, right):
    return lax.dot_general(left, right, (((0,), (0,)), ((), ())), preferred_element_type=F32)


def choose(flag, left, right):
    return lax.select(flag, left, right)


def segments(bounds, shape, axis):
    place = lax.broadcasted_iota(jnp.int32, shape, axis)
    segment = jnp.zeros(shape, jnp.int32)
    for bound in bounds:
        segment = segment + (place >= bound).astype(jnp.int32)
    return segment


def read_bounds(info, seq_count):
    bounds, total = [], 0
    for index in range(seq_count):
        total = total + info[4 + index]
        bounds.append(total)
    return bounds


def rms_parts(values, gain):
    scale = lax.rsqrt(jnp.mean(values * values, axis=-1, keepdims=True) + EPS)
    return scale, (values * scale * gain).astype(BF16)


def rms_back(values, gain, grad):
    scale = lax.rsqrt(jnp.mean(values * values, axis=-1, keepdims=True) + EPS)
    weighted = grad * gain
    inner = jnp.mean(weighted * values, axis=-1, keepdims=True)
    grad_values = scale * weighted - values * (scale * scale * scale * inner)
    grad_gain = jnp.sum(grad * values * scale, axis=0, keepdims=True)
    return grad_values, grad_gain


def head_masks(rows):
    lane = lax.broadcasted_iota(jnp.int32, (rows, PAIR), 1)
    left = (lane < PAIR // 2).astype(F32)
    return left.astype(BF16), (1.0 - left).astype(BF16)


def attend(queries, keys, values, allowed, bias_of, probs_ref, out_ref):
    q_left, q_right = head_masks(queries.shape[0])
    k_left, k_right = head_masks(keys.shape[0])
    rows = queries.shape[0]
    for pair in range(HEADS // 2):
        lanes = slice(pair * PAIR, (pair + 1) * PAIR)
        query, key, value = queries[:, lanes], keys[:, lanes], values[:, lanes]
        scores = mm_nt(jnp.concatenate([query * q_left, query * q_right], axis=0), key)
        probs = []
        for side in range(2):
            part = scores[side * rows : (side + 1) * rows]
            if bias_of is not None:
                part = part + bias_of(2 * pair + side)
            part = jnp.where(allowed, part, NEG)
            raised = jnp.exp(part - jnp.max(part, axis=-1, keepdims=True))
            weights = raised / jnp.sum(raised, axis=-1, keepdims=True)
            probs_ref[2 * pair + side] = weights
            probs.append(weights.astype(BF16))
        both = jnp.concatenate([value * k_left, value * k_right], axis=0)
        out_ref[:, lanes] = mm(jnp.concatenate(probs, axis=1), both).astype(BF16)


def attend_back(queries, keys, values, grad_out, probs_ref, dq_ref, dk_ref, dv_ref, collect):
    q_left, q_right = head_masks(queries.shape[0])
    k_left, k_right = head_masks(keys.shape[0])
    rows = queries.shape[0]
    for pair in range(HEADS // 2):
        lanes = slice(pair * PAIR, (pair + 1) * PAIR)
        query, key, value, grad = queries[:, lanes], keys[:, lanes], values[:, lanes], grad_out[:, lanes]
        grad_two = jnp.concatenate([grad * q_left, grad * q_right], axis=0)
        query_two = jnp.concatenate([query * q_left, query * q_right], axis=0)
        key_two = jnp.concatenate([key * k_left, key * k_right], axis=0)
        grad_probs = mm_nt(grad_two, value)
        probs, scores = [], []
        for side in range(2):
            weights = probs_ref[2 * pair + side]
            part = grad_probs[side * rows : (side + 1) * rows]
            inner = jnp.sum(weights * part, axis=-1, keepdims=True)
            score = (weights * (part - inner)).astype(BF16)
            if collect is not None:
                collect(2 * pair + side, score)
            probs.append(weights.astype(BF16))
            scores.append(score)
        dq_ref[:, lanes] = mm(jnp.concatenate(scores, axis=1), key_two).astype(BF16)
        dk_ref[:, lanes] = mm_tn(jnp.concatenate(scores, axis=0), query_two).astype(BF16)
        dv_ref[:, lanes] = mm_tn(jnp.concatenate(probs, axis=0), grad_two).astype(BF16)


def owners_of(info):
    core, side = info[0], info[3]
    return 2 * core + side, 2 * core + 1 - side, 2 * (1 - core) + side, 2 * (1 - core) + 1 - side


class Weights:
    def __init__(self, info, mine, theirs, weights, sems, order):
        self.weights, self.sems, self.source, self.ready = weights, sems, mine, set()
        rows = weights.shape[2]
        for place in order:
            for here, source in ((info[0] == place // 2, mine), (info[0] != place // 2, theirs)):

                @pl.when(here)
                def _(place=place, source=source):
                    pltpu.make_async_copy(
                        source.at[:, pl.ds(place % 2 * rows, rows), :], weights.at[place], sems.at[place]
                    ).start()

    def __call__(self, index):
        if index not in self.ready:
            self.ready.add(index)
            rows = self.weights.shape[2]
            pltpu.make_async_copy(
                self.source.at[:, pl.ds(0, rows), :], self.weights.at[index], self.sems.at[index]
            ).wait()
        return self.weights[index].reshape(-1, self.weights.shape[-1])


def weight_grads(info, lefts, grads, held, targets, sems):
    copies = []
    *targets, far_one, far_two = targets
    half = far_one.shape[0]
    for index, place in enumerate(owners_of(info)):
        held[index] = mm(lefts(place), grads[place]).astype(BF16).reshape(held.shape[1:])
        if index < 3:
            going = [(held.at[index], targets[index])]
        else:
            going = [(held.at[3, pl.ds(0, half)], far_one), (held.at[3, pl.ds(half, half)], far_two)]
        for source, target in going:
            copies.append(pltpu.make_async_copy(source, target, sems.at[len(copies)]))
            copies[-1].start()
    return copies


def collect_kernel(high, info, *refs):
    pieces, out, sems = refs[:-2], refs[-2], refs[-1]
    copies = []
    for step in range(high):
        owner = lax.bitwise_xor(info[1], step) * 2
        for other, place in ((0, owner + info[2]), (1, owner + 1 - info[2])):
            copy = pltpu.make_async_copy(
                pieces[2 * step + other], out.at[place], sems.at[2 * step + other]
            )
            copy.start()
            copies.append(copy)
    for copy in copies:
        copy.wait()


def self_forward(seq_count, info, tokens, gain, line, mine, theirs, q_out, k_out, v_out, probs, attn, hidden, weights, sems):
    matrix = Weights(info, mine, theirs, weights, sems, (0, 1, 2, 3))
    rows = tokens.shape[0]
    values = tokens[...].astype(F32)
    _, normed = rms_parts(values, gain[...])
    bounds = read_bounds(info, seq_count)
    allowed = segments(bounds, (rows, rows), 0) == segments(bounds, (rows, rows), 1)
    allowed = allowed & (
        lax.broadcasted_iota(jnp.int32, (rows, rows), 0) >= lax.broadcasted_iota(jnp.int32, (rows, rows), 1)
    )
    live = (segments(bounds, (rows, 1), 0) < seq_count).astype(F32)

    def bias_of(head):
        wide = jnp.broadcast_to(line[head : head + 1, :], (rows, rows))
        return pltpu.roll(wide, 0, 1, stride=1, stride_axis=0)

    q_out[...] = mm(normed, matrix(0)).astype(BF16)
    k_out[...] = mm(normed, matrix(1)).astype(BF16)
    v_out[...] = mm(normed, matrix(2)).astype(BF16)
    attend(q_out[...], k_out[...], v_out[...], allowed, bias_of, probs, attn)
    hidden[...] = values + live * mm(attn[...], matrix(3))


def cross_forward(seq_count, info, hidden_one, gain, gain_next, encoder, mine, theirs, q_out, k_out, v_out, probs, attn, hidden, normed_out, weights, sems):
    matrix = Weights(info, mine, theirs, weights, sems, (0, 1, 2, 3))
    rows, enc_rows = hidden_one.shape[0], encoder.shape[0]
    values = hidden_one[...]
    _, normed = rms_parts(values, gain[...])
    bounds = read_bounds(info, seq_count)
    clipped = jnp.minimum(segments(bounds, (rows, enc_rows), 0), seq_count - 1)
    length = enc_rows // seq_count
    place = lax.broadcasted_iota(jnp.int32, (rows, enc_rows), 1)
    key_segment = jnp.zeros((rows, enc_rows), jnp.int32)
    for index in range(1, seq_count):
        key_segment = key_segment + (place >= index * length).astype(jnp.int32)
    allowed = clipped == key_segment
    live = (segments(bounds, (rows, 1), 0) < seq_count).astype(F32)
    q_out[...] = mm(normed, matrix(0)).astype(BF16)
    k_out[...] = mm(encoder[...], matrix(1)).astype(BF16)
    v_out[...] = mm(encoder[...], matrix(2)).astype(BF16)
    attend(q_out[...], k_out[...], v_out[...], allowed, None, probs, attn)
    result = values + live * mm(attn[...], matrix(3))
    hidden[...] = result
    normed_out[...] = rms_parts(result, gain_next[...])[1]


def unpack_down(packed, owner, wide):
    sub = packed.shape[1] // 3
    return jnp.concatenate(
        [
            jnp.concatenate(
                [packed[owner, sub * g : sub * (g + 1), wide + PAIR * i : wide + PAIR * (i + 1)] for g in range(3)],
                axis=1,
            )
            for i in range(4)
        ],
        axis=0,
    )


def pack_down(target, owner, wide, values):
    sub = target.shape[1] // 3
    for i in range(4):
        for g in range(3):
            target[owner, sub * g : sub * (g + 1), wide + PAIR * i : wide + PAIR * (i + 1)] = values[
                sub * i : sub * (i + 1), PAIR * g : PAIR * (g + 1)
            ]


def feed_forward(last, seq_count, info, normed_ref, cotangent, mine_ref, theirs_ref, *refs):
    *refs, mine, theirs, g_mine, g_other, sems, out_sems = refs
    if last:
        hidden, gain, total, back, mixed, grad_hidden, grad_gain, g_mine_ref, g_other_ref = refs
    else:
        total_out, back_out, g_mine_ref, g_other_ref = refs
    flag = info[0] == 0
    rows, width = cotangent.shape
    half = width // 2
    count, _, packed = mine.shape
    wide = packed * 2 // 3
    units = wide // count
    owners = max(1, 256 // units)
    chunk = owners * units

    def parts(step, left, right, flags):
        lanes = pl.ds(step * chunk, chunk)
        places = pl.ds(step * owners, owners)
        copies = []
        for source, target in zip(left, right):
            for where in ((slice(None), slice(None), lanes), (places, slice(None), pl.ds(wide, packed - wide))):
                copies.append(
                    pltpu.make_async_copy(source.at[where], target.at[where], flags.at[step, len(copies)])
                )
        return copies

    steps = range(wide // chunk)
    coming = [parts(step, (mine_ref, theirs_ref), (mine, theirs), sems) for step in steps]
    for copies in coming:
        for copy in copies:
            copy.start()
    going = [parts(step, (g_mine, g_other), (g_mine_ref, g_other_ref), out_sems) for step in steps]
    bounds = read_bounds(info, seq_count)
    live = (segments(bounds, (rows, 1), 0) < seq_count).astype(F32)
    normed = normed_ref[...]
    normed_t = normed.T
    branch = (live * cotangent[...].astype(F32)).astype(BF16)
    left, right = branch[:, :half], branch[:, half:]
    b_mine, b_other = choose(flag, left, right), choose(flag, right, left)
    if last:
        sum_mine, sum_other, sum_back = total[0], total[1], back[...]
    else:
        sum_mine = jnp.zeros((rows, half), F32)
        sum_other = jnp.zeros((rows, half), F32)
        sum_back = jnp.zeros((rows, width), F32)
    for step in steps:
        for copy in coming[step]:
            copy.wait()
        lanes = slice(step * chunk, (step + 1) * chunk)
        places = range(step * owners, (step + 1) * owners)
        own = mine[:, :, lanes].reshape(width, chunk)
        other = theirs[:, :, lanes].reshape(width, chunk)
        down_own = jnp.concatenate([unpack_down(mine, o, wide) for o in places], axis=0)
        down_other = jnp.concatenate([unpack_down(theirs, o, wide) for o in places], axis=0)
        first, second = mm(normed, own), mm(normed, other)
        gate, up = choose(flag, first, second), choose(flag, second, first)
        inner = jnp.tanh(SQRT_2_PI * (gate + 0.044715 * (gate * gate * gate)))
        cdf = 0.5 * (1.0 + inner)
        gelu = gate * cdf
        act = (gelu * up).astype(BF16)
        sum_mine += mm(act, down_own)
        sum_other += mm(act, down_other)
        d_act = mm_nt(b_mine, down_own) + mm_nt(b_other, down_other)
        slope = cdf + 0.5 * gate * (1.0 - inner * inner) * (
            SQRT_2_PI * (1.0 + 3 * 0.044715 * (gate * gate))
        )
        d_gate = (d_act * up * slope).astype(BF16)
        d_up = (d_act * gelu).astype(BF16)
        d_own, d_other = choose(flag, d_gate, d_up), choose(flag, d_up, d_gate)
        sum_back += mm_nt(d_own, own) + mm_nt(d_other, other)
        g_mine[:, :, lanes] = mm(normed_t, d_own).astype(BF16).reshape(count, -1, chunk)
        g_other[:, :, lanes] = mm(normed_t, d_other).astype(BF16).reshape(count, -1, chunk)
        act_t = act.T
        down_grad = mm(act_t, b_mine).astype(BF16)
        down_grad_other = mm(act_t, b_other).astype(BF16)
        for index, owner in enumerate(places):
            here = slice(index * units, (index + 1) * units)
            pack_down(g_mine, owner, wide, down_grad[here])
            pack_down(g_other, owner, wide, down_grad_other[here])
        for copy in going[step]:
            copy.start()
    if last:
        outcome = jnp.concatenate(
            [choose(flag, sum_mine, sum_other), choose(flag, sum_other, sum_mine)], axis=1
        )
        mixed[...] = (hidden[...] + live * outcome).astype(BF16)
        part, term = rms_back(hidden[...], gain[...], sum_back)
        grad_hidden[...] = cotangent[...].astype(F32) + part
        grad_gain[...] = term
    else:
        total_out[0] = sum_mine
        total_out[1] = sum_other
        back_out[...] = sum_back
    for copies in going:
        for copy in copies:
            copy.wait()


def cross_backward(
    seq_count, info, grad_in, hidden_one, gain, encoder, queries, keys, values, probs, attn, mine, theirs,
    grad_out, grad_enc, grad_gain, g_own, g_side, g_core, g_far, g_far_two, weights, grads, held, sems, out_sems,
):
    matrix = Weights(info, mine, theirs, weights, sems, (3, 0, 1, 2))
    rows = hidden_one.shape[0]
    bounds = read_bounds(info, seq_count)
    live = (segments(bounds, (rows, 1), 0) < seq_count).astype(F32)
    grad = grad_in[...]
    branch = (live * grad).astype(BF16)
    _, normed = rms_parts(hidden_one[...], gain[...])
    grads[3] = branch
    normed_t, encoder_t, attn_t = normed.T, encoder[...].T, attn[...].T

    def lefts(place):
        return choose(place == 0, normed_t, choose(place == 3, attn_t, encoder_t))

    grad_attn = mm_nt(branch, matrix(3)).astype(BF16)
    attend_back(queries[...], keys[...], values[...], grad_attn, probs, grads.at[0], grads.at[1], grads.at[2], None)
    copies = weight_grads(info, lefts, grads, held, (g_own, g_side, g_core, g_far, g_far_two), out_sems)
    d_query, d_key, d_value = grads[0], grads[1], grads[2]
    grad_enc[...] = mm_nt(d_key, matrix(1)) + mm_nt(d_value, matrix(2))
    part, term = rms_back(hidden_one[...], gain[...], mm_nt(d_query, matrix(0)))
    grad_out[...] = grad + part
    grad_gain[...] = term
    for copy in copies:
        copy.wait()


def self_backward(
    seq_count, info, grad_in, tokens, gain, queries, keys, values, probs, attn, mine, theirs,
    grad_out, grad_gain, grad_line, g_own, g_side, g_core, g_far, g_far_two, weights, grads, held, sems, out_sems,
):
    matrix = Weights(info, mine, theirs, weights, sems, (3, 0, 1, 2))
    rows = tokens.shape[0]
    bounds = read_bounds(info, seq_count)
    live = (segments(bounds, (rows, 1), 0) < seq_count).astype(F32)
    grad = grad_in[...]
    branch = (live * grad).astype(BF16)
    inputs = tokens[...].astype(F32)
    _, normed = rms_parts(inputs, gain[...])
    grad_line[...] = jnp.zeros_like(grad_line)
    grads[3] = branch
    place = lax.broadcasted_iota(jnp.int32, (rows, rows), 0)
    flip = (place + lax.broadcasted_iota(jnp.int32, (rows, rows), 1) == rows - 1).astype(F32).astype(BF16)

    def collect(head, score):
        turned = pltpu.roll(mm(flip, score), 1, 1, stride=1, stride_axis=0)
        grad_line[head : head + 1, :] = jnp.sum(turned, axis=0, keepdims=True)

    grad_attn = mm_nt(branch, matrix(3)).astype(BF16)
    attend_back(
        queries[...], keys[...], values[...], grad_attn, probs, grads.at[0], grads.at[1], grads.at[2], collect
    )
    normed_t, attn_t = normed.T, attn[...].T
    copies = weight_grads(
        info,
        lambda place: choose(place == 3, attn_t, normed_t),
        grads,
        held,
        (g_own, g_side, g_core, g_far, g_far_two),
        out_sems,
    )
    d_query, d_key, d_value = grads[0], grads[1], grads[2]
    grad_normed = (
        mm_nt(d_query, matrix(0)) + mm_nt(d_key, matrix(1)) + mm_nt(d_value, matrix(2))
    )
    part, term = rms_back(inputs, gain[...], grad_normed)
    grad_out[...] = grad + part
    grad_gain[...] = term
    for copy in copies:
        copy.wait()


def finish_quarters(info, own, across, core, far, *outs):
    for place, out in enumerate(outs):
        same_core, same_side = info[0] == place // 2, info[3] == place % 2
        near = choose(same_side, own[...], across[...])
        out[...] = choose(same_core, near, choose(same_side, core[...], far[...])).astype(F32)


def finish_feed(info, one, two, there_one, there_two, gate, up, down):
    core_zero, side_zero = info[0] == 0, info[3] == 0
    rows, packed = one.shape
    wide = packed * 2 // 3
    units = down.shape[0] // 2
    half = down.shape[1] // 2
    sub = rows // 3
    pairs = ((one[...], there_one[...]), (two[...], there_two[...]))
    for part in range(2):
        first, second = pairs[part], pairs[1 - part]
        here, there = (choose(side_zero, first[k], second[k]) for k in range(2))
        for values, target, column in (
            (choose(core_zero, here, there), gate, 0),
            (choose(core_zero, there, here), up, half),
        ):
            values = values.astype(F32)
            for owner in range(wide // units):
                start = (2 * owner + part) * units
                target[:, start : start + units] = values[:, owner * units : (owner + 1) * units]
            for i in range(4):
                for g in range(3):
                    down[
                        part * units + sub * i : part * units + sub * (i + 1),
                        column + PAIR * g : column + PAIR * (g + 1),
                    ] = values[sub * g : sub * (g + 1), wide + PAIR * i : wide + PAIR * (i + 1)]


class Links:
    def __init__(self, fsdp_count, replica_count):
        self.count = fsdp_count
        self.high = fsdp_count // 2
        self.replicas = replica_count
        self.place = lax.axis_index("fsdp")
        self.mine_high = self.place // 2
        self.mine_low = self.place % 2
        self.core = lax.axis_index("replica") % 2
        self.side = lax.axis_index("replica") // 2 % 2

    def swap_replica(self, values, bit):
        pairs = [(i, i ^ bit) for i in range(self.replicas)]
        return lax.ppermute(values, "replica", pairs)

    def swap_low(self, values):
        return lax.ppermute(values, "fsdp", [(i, i ^ 1) for i in range(self.count)])

    def swap_high(self, values, step):
        return lax.ppermute(values, "fsdp", [(i, i ^ (2 * step)) for i in range(self.count)])

    def collect(self, info, pieces):
        local = pieces[0]
        nbytes = 2 * len(pieces) * local.size * 2
        return pl.pallas_call(
            functools.partial(collect_kernel, self.high),
            out_shape=jax.ShapeDtypeStruct((self.count,) + local.shape, local.dtype),
            in_specs=[SMEM] + [ANY] * len(pieces),
            out_specs=VMEM,
            scratch_shapes=[pltpu.SemaphoreType.DMA((len(pieces),))],
            compiler_params=params(16),
            cost_estimate=cost(0, nbytes),
        )(info, *pieces)

    def order(self, buckets):
        if self.high == 4 and buckets == 3:
            plan = "H02 L00 H01 L10 H03 L01 L02 H12 L20 L03 H11 H13 L11 L12 H22 L13 H21 L21 H23 L22 L23"
            steps = [(step[0] == "H", int(step[1]), int(step[2])) for step in plan.split()]
        else:
            keys = [0]
            while len(keys) < self.high:
                keys += [key | (self.high // (2 * len(keys))) for key in keys]
            steps = [(lane, index, key) for index in range(buckets) for key in keys for lane in (True, False)]
            steps = [step for step in steps if not step[0] or step[2]]
        queue = []
        for lane, index, key in steps:
            bit = key & -key
            if lane:
                queue.append(((index, key ^ bit, 0), (index, key, 0), bit))
            else:
                queue.append(((index, key, 0), (index, key, 1), 0))
        return queue

    def gather(self, locals_, window, hooks):
        got = {(index, 0, 0): local for index, local in enumerate(locals_)}
        queue = self.order(len(locals_))
        lasts = {index: max(n for n, item in enumerate(queue) if item[0][0] == index) for index in range(len(locals_))}
        hooks = {min(lasts[index] + lag, len(queue) - 2): (index, function) for index, lag, function in hooks}
        token = None
        for number, (source, target, bit) in enumerate(queue):
            values = got[source]
            if token is not None:
                values, token = after(values, token)[0], None
            if number >= window:
                old = queue[number - window][1]
                if old != source:
                    values, got[old] = lax.optimization_barrier((values, got[old]))
            got[target] = self.swap_high(values, bit) if bit else self.swap_low(values)
            if number in hooks:
                index, function = hooks[number]
                token = function(self.pieces(got, index))
        return [self.pieces(got, index) for index in range(len(locals_))]

    def pieces(self, got, index):
        return [got[index, key, side] for key in range(self.high) for side in range(2)]

    def split(self, values):
        values = values.reshape((self.high, 2) + values.shape[1:])
        return pick(values, 1 - self.mine_low, 1), pick(values, self.mine_low, 1)


class Sequence:
    def __init__(self, token):
        self.token = token

    def __call__(self, values):
        return after(values, self.token)[0]

    def mark(self, values):
        self.token = values
        return values


class Sums:
    def __init__(self, comm, sequence):
        self.comm, self.sequence = comm, sequence

    def low(self, *parts):
        parts = list(parts)
        parts[0] = self.sequence(parts[0])
        pairs = [self.comm.split(part) for part in parts]
        self.home = [pair[1] for pair in pairs]
        sent = self.sequence.mark(add(*[pair[0] for pair in pairs]))
        self.got = self.comm.swap_low(sent)
        self.bit = 0

    def step(self):
        comm = self.comm
        if not self.bit:
            total = add(self.sequence(self.got), *self.home)
            self.held = {key: pick(total, comm.mine_high ^ key, 0) for key in range(comm.high)}
            self.bit = 1
        else:
            self.receive()
            self.bit *= 2
        if self.bit >= comm.high:
            return False
        self.away = [key for key in self.held if key & self.bit]
        sent = self.sequence.mark(jnp.stack([self.held.pop(key) for key in self.away]))
        self.got = comm.swap_high(sent, self.bit)
        return True

    def receive(self):
        got = self.sequence(self.got)
        for index, key in enumerate(self.away):
            self.held[key ^ self.bit] = add(self.held[key ^ self.bit], got[index])

    def finish(self):
        while self.step():
            pass
        return self.sequence.mark(self.held[0])

    def over_replicas(self, values, bit):
        while bit < self.comm.replicas:
            values = add(values, self.comm.swap_replica(values, bit))
            bit *= 2
        return values


def add(*terms):
    return functools.reduce(jnp.add, [term.astype(F32) for term in terms]).astype(BF16)


def pick(values, index, axis):
    return lax.dynamic_index_in_dim(values, index, axis, keepdims=False)


def after(values, *tokens):
    return lax.optimization_barrier((values,) + tokens)


def per_device(
    sizes,
    tokens,
    encoded,
    lengths,
    cotangent,
    norm_self,
    q_self,
    k_self,
    v_self,
    o_self,
    bias_table,
    norm_cross,
    q_cross,
    k_cross,
    v_cross,
    o_cross,
    norm_ff,
    wi_gate,
    wi_up,
    wo_ff,
):
    count, replica_count = sizes
    comm = Links(count, replica_count)
    core_zero = comm.core == 0
    row_count, width = tokens.shape[1:]
    seq_count = lengths.shape[1]
    encoder = encoded[0].reshape(-1, width)
    enc_rows = encoder.shape[0]
    rows = q_self.shape[0]
    hidden_units = wi_gate.shape[1]
    down_rows = wo_ff.shape[0]
    half = width // 2
    info = jnp.concatenate(
        [jnp.stack([comm.core, comm.mine_high, comm.mine_low, comm.side]), lengths[0]]
    ).astype(jnp.int32)
    small = jnp.concatenate([norm_self, norm_cross, norm_ff, bias_table.reshape(-1)])
    small_count = small.shape[0]
    small = jnp.pad(small[None], ((0, 15), (0, width - small_count)))

    units = down_rows // 2
    side_zero = comm.side == 0
    wide = jnp.where(core_zero, wi_gate, wi_up).reshape(rows, count, 2, units)

    wide = pick(wide, comm.side, 2).reshape(rows, -1)
    down = pick(wo_ff.reshape(2, units, width), comm.side, 0)
    down = jnp.where(core_zero, down[:, :half], down[:, half:])
    down = down.reshape(4, units // 4, 3, PAIR).transpose(2, 1, 0, 3).reshape(rows, -1)
    feed_local = jnp.concatenate([wide, down], axis=1)
    first_local = jnp.concatenate(
        [jnp.where(core_zero, q_self, v_self), jnp.where(core_zero, k_self, o_self), small]
    )
    second_local = jnp.concatenate(
        [jnp.where(core_zero, q_cross, v_cross), jnp.where(core_zero, k_cross, o_cross)]
    )
    feed_pieces, first_pieces, second_pieces = comm.gather(
        [feed_local, first_local, second_local], 4, []
    )
    feed_one, first_mine = comm.collect(info, feed_pieces), comm.collect(info, first_pieces)
    feed_two = comm.swap_replica(feed_one, 2)
    feed_one_theirs = comm.swap_replica(feed_one, 1)
    first_theirs = comm.swap_replica(first_mine, 1)

    vectors = first_mine[:, 2 * rows, :small_count].astype(F32)
    gain_one = vectors[:, :rows].reshape(1, -1)
    gain_two = vectors[:, rows : 2 * rows].reshape(1, -1)
    gain_three = vectors[:, 2 * rows : 3 * rows].reshape(1, -1)
    table = vectors[:, 3 * rows :].reshape(-1, HEADS)
    turned = jnp.asarray((-np.arange(row_count)) % row_count, jnp.int32)
    bucket_hot = (
        bucket_of(turned)[:, None] == lax.iota(jnp.int32, table.shape[0])[None, :]
    ).astype(F32)
    line = jnp.dot(bucket_hot, table, precision=lax.Precision.HIGHEST).T
    line = jnp.pad(line, ((0, 16 - HEADS), (0, 0)))

    def shape(*dims, dtype=BF16):
        return jax.ShapeDtypeStruct(dims, dtype)

    act = shape(row_count, width)
    act_enc = shape(enc_rows, width)
    act32 = shape(row_count, width, dtype=F32)
    vec32 = shape(1, width, dtype=F32)
    weight_scratch = pltpu.VMEM((4, count, rows, width), BF16)
    sems = pltpu.SemaphoreType.DMA((4,))
    weight_bytes = 4 * count * rows * width * 2
    pair_flops = 2 * row_count * width * width
    attn_scratch = pltpu.VMEM((4, row_count, width), BF16)

    tokens_here = tokens[0]
    queries, keys, values, probs, attn_one, hidden_one = pl.pallas_call(
        functools.partial(self_forward, seq_count),
        out_shape=(act, act, act, shape(HEADS, row_count, row_count, dtype=F32), act, act32),
        in_specs=[SMEM, VMEM, VMEM, VMEM] + [ANY] * 2,
        out_specs=[VMEM] * 6,
        scratch_shapes=[weight_scratch, sems],
        compiler_params=params(),
        cost_estimate=cost(5 * pair_flops, weight_bytes),
    )(info, tokens_here, gain_one, line, first_mine, first_theirs)

    second_mine = comm.collect(info, second_pieces)
    second_theirs = comm.swap_replica(second_mine, 1)
    feed_two_theirs = comm.swap_replica(feed_two, 1)
    queries_c, keys_c, values_c, probs_c, attn_two, hidden_two, normed_three = pl.pallas_call(
        functools.partial(cross_forward, seq_count),
        out_shape=(act, act_enc, act_enc, shape(HEADS, row_count, enc_rows, dtype=F32), act, act32, act),
        in_specs=[SMEM, VMEM, VMEM, VMEM, VMEM] + [ANY] * 2,
        out_specs=[VMEM] * 7,
        scratch_shapes=[weight_scratch, sems],
        compiler_params=params(),
        cost_estimate=cost(5 * pair_flops, weight_bytes),
    )(info, hidden_one, gain_two, gain_three, encoder, second_mine, second_theirs)

    packed = shape(*feed_one.shape)
    feed_steps = pltpu.SemaphoreType.DMA((count, 4))
    feed_scratch = [pltpu.VMEM(feed_one.shape, BF16)] * 4 + [feed_steps, feed_steps]
    feed_cost = cost(9 * row_count * width * hidden_units, 12 * width * hidden_units)
    total, back, g_one, g_one_other = pl.pallas_call(
        functools.partial(feed_forward, False, seq_count),
        out_shape=(shape(2, row_count, half, dtype=F32), act32, packed, packed),
        in_specs=[SMEM, VMEM, VMEM, ANY, ANY],
        out_specs=[VMEM, VMEM, ANY, ANY],
        scratch_shapes=feed_scratch,
        compiler_params=params(),
        cost_estimate=feed_cost,
    )(info, normed_three, cotangent[0], feed_one, feed_one_theirs)
    mixed, grad_hidden_two, grad_norm_three, g_two, g_two_other = pl.pallas_call(
        functools.partial(feed_forward, True, seq_count),
        out_shape=(act, act32, vec32, packed, packed),
        in_specs=[SMEM, VMEM, VMEM, ANY, ANY] + [VMEM] * 4,
        out_specs=[VMEM] * 3 + [ANY] * 2,
        scratch_shapes=feed_scratch,
        compiler_params=params(),
        cost_estimate=feed_cost,
    )(info, normed_three, cotangent[0], feed_two, feed_two_theirs, hidden_two, gain_three, total, back)

    sequence = Sequence(grad_norm_three)
    one, two, second, first = (Sums(comm, sequence) for _ in range(4))
    one_got = comm.swap_replica(g_one_other, 1)
    two_got = comm.swap_replica(g_two_other, 1)
    one.low(g_one, one_got)
    grad_hidden_two = sequence(grad_hidden_two)

    grads = shape(count, rows, width)
    grads_half = shape(count // 2, rows, width)
    out_sems = pltpu.SemaphoreType.DMA((5,))
    grad_hidden_one, grad_encoder, grad_norm_two, *g_second = pl.pallas_call(
        functools.partial(cross_backward, seq_count),
        out_shape=(act32, shape(enc_rows, width, dtype=F32), vec32) + (grads,) * 3 + (grads_half,) * 2,
        in_specs=[SMEM] + [VMEM] * 9 + [ANY] * 2,
        out_specs=[VMEM] * 3 + [ANY] * 5,
        scratch_shapes=[weight_scratch, attn_scratch, weight_scratch, sems, out_sems],
        compiler_params=params(),
        cost_estimate=cost(10 * pair_flops, 2 * weight_bytes),
    )(
        info, grad_hidden_two, hidden_one, gain_two, encoder, queries_c, keys_c, values_c, probs_c, attn_two,
        second_mine, second_theirs,
    )
    def across(g_own, g_side, g_core, *g_far):
        from_far = [comm.swap_replica(part, 1) for part in g_far]
        from_core = comm.swap_replica(g_core, 1)

        def finish():
            from_far[0] = sequence(from_far[0])
            side = sequence.mark(add(jnp.concatenate(from_far), g_side))
            return g_own, from_core, comm.swap_replica(side, 2)

        return finish

    sequence.mark(grad_norm_two)
    two.low(g_two, two_got)
    second_parts = across(*g_second)()
    grad_hidden_one = sequence(grad_hidden_one)

    grad_inputs, grad_norm_one, grad_line, *g_first = pl.pallas_call(
        functools.partial(self_backward, seq_count),
        out_shape=(act32, vec32, shape(16, row_count, dtype=F32)) + (grads,) * 3 + (grads_half,) * 2,
        in_specs=[SMEM] + [VMEM] * 8 + [ANY] * 2,
        out_specs=[VMEM] * 3 + [ANY] * 5,
        scratch_shapes=[weight_scratch, attn_scratch, weight_scratch, sems, out_sems],
        compiler_params=params(),
        cost_estimate=cost(10 * pair_flops, 2 * weight_bytes),
    )(
        info, grad_hidden_one, tokens_here, gain_one, queries, keys, values, probs, attn_one,
        first_mine, first_theirs,
    )
    sequence.mark(grad_norm_one)
    first_across = across(*g_first)
    one.step()
    first_parts = first_across()
    second.low(*second_parts)
    grad_table = jnp.dot(grad_line[:HEADS], bucket_hot, precision=lax.Precision.HIGHEST).T
    table_row = jnp.pad(grad_table.reshape(1, -1), ((0, 0), (0, width - grad_table.size)))
    vectors = jnp.concatenate([grad_norm_one, grad_norm_two, grad_norm_three, table_row])
    steps = [("replica", 1 << k) for k in range(replica_count.bit_length() - 1)]
    steps += [("fsdp", 1 << k) for k in range(count.bit_length() - 1)]

    def small_step():
        axis, bit = steps.pop(0)
        size = replica_count if axis == "replica" else count
        return lax.ppermute(sequence(vectors), axis, [(i, i ^ bit) for i in range(size)])

    def small_sum(got):
        return vectors + sequence(got)

    got = small_step()
    one.step()
    two.step()
    vectors = small_sum(got)
    got = small_step()
    second.step()
    first.low(*first_parts)
    vectors = small_sum(got)
    got = small_step()
    one_part = one.finish()
    two.step()
    second.step()
    vectors = small_sum(got)
    got = small_step()
    first.step()
    vectors = small_sum(got)
    got = small_step()
    two_part = two.finish()
    one_cross, two_cross = comm.swap_replica(two_part, 2), comm.swap_replica(one_part, 2)
    first.step()
    second_sum = second.over_replicas(second.finish(), 4)
    second_cross, second_core = comm.swap_replica(second_sum, 2), comm.swap_replica(second_sum, 1)
    one_sum = one.over_replicas(add(one_part, sequence(one_cross)), 4)
    two_sum = two.over_replicas(add(two_part, two_cross), 4)
    sequence.mark(two_sum)
    there = comm.swap_replica(one_sum, 1), comm.swap_replica(two_sum, 1)
    vectors = small_sum(got)
    while steps:
        vectors = small_sum(small_step())
    first_sum = first.over_replicas(first.finish(), 4)
    first_cross, first_core = comm.swap_replica(first_sum, 2), comm.swap_replica(first_sum, 1)
    second_far = comm.swap_replica(second_cross, 1)
    first_far = None

    full = jax.ShapeDtypeStruct((rows, width), F32)

    def four(*arrays):
        return pl.pallas_call(
            finish_quarters,
            out_shape=(full,) * 4,
            in_specs=[SMEM] + [VMEM] * 4,
            out_specs=[VMEM] * 4,
            compiler_params=params(16),
            cost_estimate=cost(0, 24 * rows * width),
        )(info, *arrays)

    owned = lax.dynamic_slice(vectors, (0, comm.place * rows), (3, rows))
    table_size = bias_table.size
    owned_table = lax.dynamic_slice(vectors[3], (comm.place * table_size,), (table_size,))

    second = four(second_sum, second_cross, second_core, second_far)
    if units % PAIR == 0:
        grad_gate, grad_up, grad_down = pl.pallas_call(
            finish_feed,
            out_shape=(
                shape(rows, hidden_units, dtype=F32), shape(rows, hidden_units, dtype=F32),
                shape(down_rows, width, dtype=F32),
            ),
            in_specs=[SMEM] + [VMEM] * 4,
            out_specs=[VMEM] * 3,
            compiler_params=params(16),
            cost_estimate=cost(0, 36 * rows * hidden_units),
        )(info, one_sum, two_sum, *there)
    else:
        def by_side(one, two):
            return jnp.where(side_zero, one, two), jnp.where(side_zero, two, one)

        here, there = by_side(one_sum, two_sum), by_side(*there)
        wide_units = hidden_units // 2

        def wide_grad(parts):
            parts = [part[:, :wide_units].reshape(rows, count, 1, units) for part in parts]
            return jnp.concatenate(parts, axis=2).reshape(rows, hidden_units).astype(F32)

        def down_grad(parts):
            parts = [
                part[:, wide_units:].reshape(3, units // 4, 4, PAIR).transpose(2, 1, 0, 3).reshape(units, half)
                for part in parts
            ]
            return jnp.concatenate(parts, axis=0)

        low = [jnp.where(core_zero, one, two) for one, two in zip(here, there)]
        high = [jnp.where(core_zero, two, one) for one, two in zip(here, there)]
        grad_down = jnp.concatenate([down_grad(low), down_grad(high)], axis=1).astype(F32)
        grad_gate, grad_up = wide_grad(low), wide_grad(high)
    first_far = comm.swap_replica(after(first_cross, grad_gate, grad_up, grad_down, *second)[0], 1)
    first = four(first_sum, first_cross, first_core, first_far)
    return (
        mixed[None],
        grad_inputs[None],
        grad_encoder.reshape(encoded.shape),
        owned[0],
        first[0],
        first[1],
        first[2],
        first[3],
        owned_table.reshape(bias_table.shape),
        owned[1],
        second[0],
        second[1],
        second[2],
        second[3],
        owned[2],
        grad_gate,
        grad_up,
        grad_down,
    )


def solution(mesh):
    slots = P(("replica", "fsdp"), None, None)
    slots_four = P(("replica", "fsdp"), None, None, None)
    vector, matrix = P("fsdp"), P("fsdp", None)
    weights = (
        (vector,) + (matrix,) * 5 + (vector,) + (matrix,) * 4 + (vector,) + (matrix,) * 3
    )
    return jax.shard_map(
        functools.partial(per_device, (mesh.shape["fsdp"], mesh.shape["replica"])),
        mesh=mesh,
        in_specs=(slots, slots_four, P(("replica", "fsdp"), None), slots) + weights,
        out_specs=(slots, slots, slots_four) + weights,
        check_vma=False,
    )
```

```python
import functools
import math

import jax
import jax.numpy as jnp
import numpy as np
from jax import lax
from jax.experimental import pallas as pl
from jax.experimental.pallas import tpu as pltpu
from jax.sharding import PartitionSpec as P

HEADS = 12
PAIR = 128
EPS = 1e-06
NEG = -1e30
SQRT_2_PI = math.sqrt(2 / math.pi)
bucket_edges = np.array([math.ceil(16 * 8 ** (k / 16)) for k in range(1, 16)], np.int32)

F32 = jnp.float32
BF16 = jnp.bfloat16
VMEM = pl.BlockSpec(memory_space=pltpu.VMEM)
SMEM = pl.BlockSpec(memory_space=pltpu.SMEM)
ANY = pl.BlockSpec(memory_space=pl.ANY)


def params(limit=56):
    return pltpu.CompilerParams(vmem_limit_bytes=limit * 1024 * 1024)


def cost(flops, nbytes):
    return pl.CostEstimate(flops=flops, bytes_accessed=nbytes, transcendentals=0)


def bucket_of(offset):
    distance = jnp.maximum(offset, 0)
    counted = jnp.sum((distance[..., None] >= jnp.asarray(bucket_edges)).astype(jnp.int32), axis=-1)
    return jnp.where(distance < 16, distance, 16 + counted)


def mm(left, right):
    return jnp.dot(left, right, preferred_element_type=F32)


def mm_nt(left, right):
    return lax.dot_general(left, right, (((1,), (1,)), ((), ())), preferred_element_type=F32)


def mm_tn(left, right):
    return lax.dot_general(left, right, (((0,), (0,)), ((), ())), preferred_element_type=F32)


def choose(flag, left, right):
    return lax.select(flag, left, right)


def segments(bounds, shape, axis):
    place = lax.broadcasted_iota(jnp.int32, shape, axis)
    segment = jnp.zeros(shape, jnp.int32)
    for bound in bounds:
        segment = segment + (place >= bound).astype(jnp.int32)
    return segment


def read_bounds(info, seq_count):
    bounds, total = [], 0
    for index in range(seq_count):
        total = total + info[4 + index]
        bounds.append(total)
    return bounds


def rms_parts(values, gain):
    scale = lax.rsqrt(jnp.mean(values * values, axis=-1, keepdims=True) + EPS)
    return scale, (values * scale * gain).astype(BF16)


def rms_back(values, gain, grad):
    scale = lax.rsqrt(jnp.mean(values * values, axis=-1, keepdims=True) + EPS)
    weighted = grad * gain
    inner = jnp.mean(weighted * values, axis=-1, keepdims=True)
    grad_values = scale * weighted - values * (scale * scale * scale * inner)
    grad_gain = jnp.sum(grad * values * scale, axis=0, keepdims=True)
    return grad_values, grad_gain


def head_masks(rows):
    lane = lax.broadcasted_iota(jnp.int32, (rows, PAIR), 1)
    left = (lane < PAIR // 2).astype(F32)
    return left.astype(BF16), (1.0 - left).astype(BF16)


def attend(queries, keys, values, allowed, bias_of, probs_ref, out_ref):
    q_left, q_right = head_masks(queries.shape[0])
    k_left, k_right = head_masks(keys.shape[0])
    rows = queries.shape[0]
    for pair in range(HEADS // 2):
        lanes = slice(pair * PAIR, (pair + 1) * PAIR)
        query, key, value = queries[:, lanes], keys[:, lanes], values[:, lanes]
        scores = mm_nt(jnp.concatenate([query * q_left, query * q_right], axis=0), key)
        probs = []
        for side in range(2):
            part = scores[side * rows : (side + 1) * rows]
            if bias_of is not None:
                part = part + bias_of(2 * pair + side)
            part = jnp.where(allowed, part, NEG)
            raised = jnp.exp(part - jnp.max(part, axis=-1, keepdims=True))
            weights = raised / jnp.sum(raised, axis=-1, keepdims=True)
            probs_ref[2 * pair + side] = weights
            probs.append(weights.astype(BF16))
        both = jnp.concatenate([value * k_left, value * k_right], axis=0)
        out_ref[:, lanes] = mm(jnp.concatenate(probs, axis=1), both).astype(BF16)


def attend_back(queries, keys, values, grad_out, probs_ref, dq_ref, dk_ref, dv_ref, collect):
    q_left, q_right = head_masks(queries.shape[0])
    k_left, k_right = head_masks(keys.shape[0])
    rows = queries.shape[0]
    for pair in range(HEADS // 2):
        lanes = slice(pair * PAIR, (pair + 1) * PAIR)
        query, key, value, grad = queries[:, lanes], keys[:, lanes], values[:, lanes], grad_out[:, lanes]
        grad_two = jnp.concatenate([grad * q_left, grad * q_right], axis=0)
        query_two = jnp.concatenate([query * q_left, query * q_right], axis=0)
        key_two = jnp.concatenate([key * k_left, key * k_right], axis=0)
        grad_probs = mm_nt(grad_two, value)
        probs, scores = [], []
        for side in range(2):
            weights = probs_ref[2 * pair + side]
            part = grad_probs[side * rows : (side + 1) * rows]
            inner = jnp.sum(weights * part, axis=-1, keepdims=True)
            score = (weights * (part - inner)).astype(BF16)
            if collect is not None:
                collect(2 * pair + side, score)
            probs.append(weights.astype(BF16))
            scores.append(score)
        dq_ref[:, lanes] = mm(jnp.concatenate(scores, axis=1), key_two).astype(BF16)
        dk_ref[:, lanes] = mm_tn(jnp.concatenate(scores, axis=0), query_two).astype(BF16)
        dv_ref[:, lanes] = mm_tn(jnp.concatenate(probs, axis=0), grad_two).astype(BF16)


def owners_of(info):
    core, side = info[0], info[3]
    return 2 * core + side, 2 * core + 1 - side, 2 * (1 - core) + side, 2 * (1 - core) + 1 - side


class Weights:
    def __init__(self, info, mine, theirs, weights, sems, order):
        self.weights, self.sems, self.source, self.ready = weights, sems, mine, set()
        rows = weights.shape[2]
        for place in order:
            for here, source in ((info[0] == place // 2, mine), (info[0] != place // 2, theirs)):

                @pl.when(here)
                def _(place=place, source=source):
                    pltpu.make_async_copy(
                        source.at[:, pl.ds(place % 2 * rows, rows), :], weights.at[place], sems.at[place]
                    ).start()

    def __call__(self, index):
        if index not in self.ready:
            self.ready.add(index)
            rows = self.weights.shape[2]
            pltpu.make_async_copy(
                self.source.at[:, pl.ds(0, rows), :], self.weights.at[index], self.sems.at[index]
            ).wait()
        return self.weights[index].reshape(-1, self.weights.shape[-1])


def weight_grads(info, lefts, grads, held, targets, sems):
    copies = []
    *targets, far_one, far_two = targets
    half = far_one.shape[0]
    for index, place in enumerate(owners_of(info)):
        held[index] = mm(lefts(place), grads[place]).astype(BF16).reshape(held.shape[1:])
        if index < 3:
            going = [(held.at[index], targets[index])]
        else:
            going = [(held.at[3, pl.ds(0, half)], far_one), (held.at[3, pl.ds(half, half)], far_two)]
        for source, target in going:
            copies.append(pltpu.make_async_copy(source, target, sems.at[len(copies)]))
            copies[-1].start()
    return copies


def collect_kernel(high, info, *refs):
    pieces, out, sems = refs[:-2], refs[-2], refs[-1]
    copies = []
    for step in range(high):
        owner = lax.bitwise_xor(info[1], step) * 2
        for other, place in ((0, owner + info[2]), (1, owner + 1 - info[2])):
            copy = pltpu.make_async_copy(
                pieces[2 * step + other], out.at[place], sems.at[2 * step + other]
            )
            copy.start()
            copies.append(copy)
    for copy in copies:
        copy.wait()


def self_forward(seq_count, info, tokens, gain, line, mine, theirs, q_out, k_out, v_out, probs, attn, hidden, weights, sems):
    matrix = Weights(info, mine, theirs, weights, sems, (0, 1, 2, 3))
    rows = tokens.shape[0]
    values = tokens[...].astype(F32)
    _, normed = rms_parts(values, gain[...])
    bounds = read_bounds(info, seq_count)
    allowed = segments(bounds, (rows, rows), 0) == segments(bounds, (rows, rows), 1)
    allowed = allowed & (
        lax.broadcasted_iota(jnp.int32, (rows, rows), 0) >= lax.broadcasted_iota(jnp.int32, (rows, rows), 1)
    )
    live = (segments(bounds, (rows, 1), 0) < seq_count).astype(F32)

    def bias_of(head):
        wide = jnp.broadcast_to(line[head : head + 1, :], (rows, rows))
        return pltpu.roll(wide, 0, 1, stride=1, stride_axis=0)

    q_out[...] = mm(normed, matrix(0)).astype(BF16)
    k_out[...] = mm(normed, matrix(1)).astype(BF16)
    v_out[...] = mm(normed, matrix(2)).astype(BF16)
    attend(q_out[...], k_out[...], v_out[...], allowed, bias_of, probs, attn)
    hidden[...] = values + live * mm(attn[...], matrix(3))


def cross_forward(seq_count, info, hidden_one, gain, gain_next, encoder, mine, theirs, q_out, k_out, v_out, probs, attn, hidden, normed_out, weights, sems):
    matrix = Weights(info, mine, theirs, weights, sems, (0, 1, 2, 3))
    rows, enc_rows = hidden_one.shape[0], encoder.shape[0]
    values = hidden_one[...]
    _, normed = rms_parts(values, gain[...])
    bounds = read_bounds(info, seq_count)
    clipped = jnp.minimum(segments(bounds, (rows, enc_rows), 0), seq_count - 1)
    length = enc_rows // seq_count
    place = lax.broadcasted_iota(jnp.int32, (rows, enc_rows), 1)
    key_segment = jnp.zeros((rows, enc_rows), jnp.int32)
    for index in range(1, seq_count):
        key_segment = key_segment + (place >= index * length).astype(jnp.int32)
    allowed = clipped == key_segment
    live = (segments(bounds, (rows, 1), 0) < seq_count).astype(F32)
    q_out[...] = mm(normed, matrix(0)).astype(BF16)
    k_out[...] = mm(encoder[...], matrix(1)).astype(BF16)
    v_out[...] = mm(encoder[...], matrix(2)).astype(BF16)
    attend(q_out[...], k_out[...], v_out[...], allowed, None, probs, attn)
    result = values + live * mm(attn[...], matrix(3))
    hidden[...] = result
    normed_out[...] = rms_parts(result, gain_next[...])[1]


def unpack_down(packed, owner, wide):
    sub = packed.shape[1] // 3
    return jnp.concatenate(
        [
            jnp.concatenate(
                [packed[owner, sub * g : sub * (g + 1), wide + PAIR * i : wide + PAIR * (i + 1)] for g in range(3)],
                axis=1,
            )
            for i in range(4)
        ],
        axis=0,
    )


def pack_down(target, owner, wide, values):
    sub = target.shape[1] // 3
    for i in range(4):
        for g in range(3):
            target[owner, sub * g : sub * (g + 1), wide + PAIR * i : wide + PAIR * (i + 1)] = values[
                sub * i : sub * (i + 1), PAIR * g : PAIR * (g + 1)
            ]


def feed_forward(last, seq_count, info, normed_ref, cotangent, mine_ref, theirs_ref, *refs):
    *refs, mine, theirs, g_mine, g_other, sems, out_sems = refs
    if last:
        hidden, gain, total, back, mixed, grad_hidden, grad_gain, g_mine_ref, g_other_ref = refs
    else:
        total_out, back_out, g_mine_ref, g_other_ref = refs
    flag = info[0] == 0
    rows, width = cotangent.shape
    half = width // 2
    count, _, packed = mine.shape
    wide = packed * 2 // 3
    units = wide // count
    owners = max(1, 256 // units)
    chunk = owners * units

    def parts(step, left, right, flags):
        lanes = pl.ds(step * chunk, chunk)
        places = pl.ds(step * owners, owners)
        copies = []
        for source, target in zip(left, right):
            for where in ((slice(None), slice(None), lanes), (places, slice(None), pl.ds(wide, packed - wide))):
                copies.append(
                    pltpu.make_async_copy(source.at[where], target.at[where], flags.at[step, len(copies)])
                )
        return copies

    steps = range(wide // chunk)
    coming = [parts(step, (mine_ref, theirs_ref), (mine, theirs), sems) for step in steps]
    for copies in coming:
        for copy in copies:
            copy.start()
    going = [parts(step, (g_mine, g_other), (g_mine_ref, g_other_ref), out_sems) for step in steps]
    bounds = read_bounds(info, seq_count)
    live = (segments(bounds, (rows, 1), 0) < seq_count).astype(F32)
    normed = normed_ref[...]
    normed_t = normed.T
    branch = (live * cotangent[...].astype(F32)).astype(BF16)
    left, right = branch[:, :half], branch[:, half:]
    b_mine, b_other = choose(flag, left, right), choose(flag, right, left)
    if last:
        sum_mine, sum_other, sum_back = total[0], total[1], back[...]
    else:
        sum_mine = jnp.zeros((rows, half), F32)
        sum_other = jnp.zeros((rows, half), F32)
        sum_back = jnp.zeros((rows, width), F32)
    for step in steps:
        for copy in coming[step]:
            copy.wait()
        lanes = slice(step * chunk, (step + 1) * chunk)
        places = range(step * owners, (step + 1) * owners)
        own = mine[:, :, lanes].reshape(width, chunk)
        other = theirs[:, :, lanes].reshape(width, chunk)
        down_own = jnp.concatenate([unpack_down(mine, o, wide) for o in places], axis=0)
        down_other = jnp.concatenate([unpack_down(theirs, o, wide) for o in places], axis=0)
        first, second = mm(normed, own), mm(normed, other)
        gate, up = choose(flag, first, second), choose(flag, second, first)
        inner = jnp.tanh(SQRT_2_PI * (gate + 0.044715 * (gate * gate * gate)))
        cdf = 0.5 * (1.0 + inner)
        gelu = gate * cdf
        act = (gelu * up).astype(BF16)
        sum_mine += mm(act, down_own)
        sum_other += mm(act, down_other)
        d_act = mm_nt(b_mine, down_own) + mm_nt(b_other, down_other)
        slope = cdf + 0.5 * gate * (1.0 - inner * inner) * (
            SQRT_2_PI * (1.0 + 3 * 0.044715 * (gate * gate))
        )
        d_gate = (d_act * up * slope).astype(BF16)
        d_up = (d_act * gelu).astype(BF16)
        d_own, d_other = choose(flag, d_gate, d_up), choose(flag, d_up, d_gate)
        sum_back += mm_nt(d_own, own) + mm_nt(d_other, other)
        g_mine[:, :, lanes] = mm(normed_t, d_own).astype(BF16).reshape(count, -1, chunk)
        g_other[:, :, lanes] = mm(normed_t, d_other).astype(BF16).reshape(count, -1, chunk)
        act_t = act.T
        down_grad = mm(act_t, b_mine).astype(BF16)
        down_grad_other = mm(act_t, b_other).astype(BF16)
        for index, owner in enumerate(places):
            here = slice(index * units, (index + 1) * units)
            pack_down(g_mine, owner, wide, down_grad[here])
            pack_down(g_other, owner, wide, down_grad_other[here])
        for copy in going[step]:
            copy.start()
    if last:
        outcome = jnp.concatenate(
            [choose(flag, sum_mine, sum_other), choose(flag, sum_other, sum_mine)], axis=1
        )
        mixed[...] = (hidden[...] + live * outcome).astype(BF16)
        part, term = rms_back(hidden[...], gain[...], sum_back)
        grad_hidden[...] = cotangent[...].astype(F32) + part
        grad_gain[...] = term
    else:
        total_out[0] = sum_mine
        total_out[1] = sum_other
        back_out[...] = sum_back
    for copies in going:
        for copy in copies:
            copy.wait()


def cross_backward(
    seq_count, info, grad_in, hidden_one, gain, encoder, queries, keys, values, probs, attn, mine, theirs,
    grad_out, grad_enc, grad_gain, g_own, g_side, g_core, g_far, g_far_two, weights, grads, held, sems, out_sems,
):
    matrix = Weights(info, mine, theirs, weights, sems, (3, 0, 1, 2))
    rows = hidden_one.shape[0]
    bounds = read_bounds(info, seq_count)
    live = (segments(bounds, (rows, 1), 0) < seq_count).astype(F32)
    grad = grad_in[...]
    branch = (live * grad).astype(BF16)
    _, normed = rms_parts(hidden_one[...], gain[...])
    grads[3] = branch
    normed_t, encoder_t, attn_t = normed.T, encoder[...].T, attn[...].T

    def lefts(place):
        return choose(place == 0, normed_t, choose(place == 3, attn_t, encoder_t))

    grad_attn = mm_nt(branch, matrix(3)).astype(BF16)
    attend_back(queries[...], keys[...], values[...], grad_attn, probs, grads.at[0], grads.at[1], grads.at[2], None)
    copies = weight_grads(info, lefts, grads, held, (g_own, g_side, g_core, g_far, g_far_two), out_sems)
    d_query, d_key, d_value = grads[0], grads[1], grads[2]
    grad_enc[...] = mm_nt(d_key, matrix(1)) + mm_nt(d_value, matrix(2))
    part, term = rms_back(hidden_one[...], gain[...], mm_nt(d_query, matrix(0)))
    grad_out[...] = grad + part
    grad_gain[...] = term
    for copy in copies:
        copy.wait()


def self_backward(
    seq_count, info, grad_in, tokens, gain, queries, keys, values, probs, attn, mine, theirs,
    grad_out, grad_gain, grad_line, g_own, g_side, g_core, g_far, g_far_two, weights, grads, held, sems, out_sems,
):
    matrix = Weights(info, mine, theirs, weights, sems, (3, 0, 1, 2))
    rows = tokens.shape[0]
    bounds = read_bounds(info, seq_count)
    live = (segments(bounds, (rows, 1), 0) < seq_count).astype(F32)
    grad = grad_in[...]
    branch = (live * grad).astype(BF16)
    inputs = tokens[...].astype(F32)
    _, normed = rms_parts(inputs, gain[...])
    grad_line[...] = jnp.zeros_like(grad_line)
    grads[3] = branch
    place = lax.broadcasted_iota(jnp.int32, (rows, rows), 0)
    flip = (place + lax.broadcasted_iota(jnp.int32, (rows, rows), 1) == rows - 1).astype(F32).astype(BF16)

    def collect(head, score):
        turned = pltpu.roll(mm(flip, score), 1, 1, stride=1, stride_axis=0)
        grad_line[head : head + 1, :] = jnp.sum(turned, axis=0, keepdims=True)

    grad_attn = mm_nt(branch, matrix(3)).astype(BF16)
    attend_back(
        queries[...], keys[...], values[...], grad_attn, probs, grads.at[0], grads.at[1], grads.at[2], collect
    )
    normed_t, attn_t = normed.T, attn[...].T
    copies = weight_grads(
        info,
        lambda place: choose(place == 3, attn_t, normed_t),
        grads,
        held,
        (g_own, g_side, g_core, g_far, g_far_two),
        out_sems,
    )
    d_query, d_key, d_value = grads[0], grads[1], grads[2]
    grad_normed = (
        mm_nt(d_query, matrix(0)) + mm_nt(d_key, matrix(1)) + mm_nt(d_value, matrix(2))
    )
    part, term = rms_back(inputs, gain[...], grad_normed)
    grad_out[...] = grad + part
    grad_gain[...] = term
    for copy in copies:
        copy.wait()


def finish_quarters(info, own, across, core, far, *outs):
    for place, out in enumerate(outs):
        same_core, same_side = info[0] == place // 2, info[3] == place % 2
        near = choose(same_side, own[...], across[...])
        out[...] = choose(same_core, near, choose(same_side, core[...], far[...])).astype(F32)


def finish_feed(info, one, two, there_one, there_two, gate, up, down):
    core_zero, side_zero = info[0] == 0, info[3] == 0
    rows, packed = one.shape
    wide = packed * 2 // 3
    units = down.shape[0] // 2
    half = down.shape[1] // 2
    sub = rows // 3
    pairs = ((one[...], there_one[...]), (two[...], there_two[...]))
    for part in range(2):
        first, second = pairs[part], pairs[1 - part]
        here, there = (choose(side_zero, first[k], second[k]) for k in range(2))
        for values, target, column in (
            (choose(core_zero, here, there), gate, 0),
            (choose(core_zero, there, here), up, half),
        ):
            values = values.astype(F32)
            for owner in range(wide // units):
                start = (2 * owner + part) * units
                target[:, start : start + units] = values[:, owner * units : (owner + 1) * units]
            for i in range(4):
                for g in range(3):
                    down[
                        part * units + sub * i : part * units + sub * (i + 1),
                        column + PAIR * g : column + PAIR * (g + 1),
                    ] = values[sub * g : sub * (g + 1), wide + PAIR * i : wide + PAIR * (i + 1)]


class Links:
    def __init__(self, fsdp_count, replica_count):
        self.count = fsdp_count
        self.high = fsdp_count // 2
        self.replicas = replica_count
        self.place = lax.axis_index("fsdp")
        self.mine_high = self.place // 2
        self.mine_low = self.place % 2
        self.core = lax.axis_index("replica") % 2
        self.side = lax.axis_index("replica") // 2 % 2

    def swap_replica(self, values, bit):
        pairs = [(i, i ^ bit) for i in range(self.replicas)]
        return lax.ppermute(values, "replica", pairs)

    def swap_low(self, values):
        return lax.ppermute(values, "fsdp", [(i, i ^ 1) for i in range(self.count)])

    def swap_high(self, values, step):
        return lax.ppermute(values, "fsdp", [(i, i ^ (2 * step)) for i in range(self.count)])

    def collect(self, info, pieces):
        local = pieces[0]
        nbytes = 2 * len(pieces) * local.size * 2
        return pl.pallas_call(
            functools.partial(collect_kernel, self.high),
            out_shape=jax.ShapeDtypeStruct((self.count,) + local.shape, local.dtype),
            in_specs=[SMEM] + [ANY] * len(pieces),
            out_specs=VMEM,
            scratch_shapes=[pltpu.SemaphoreType.DMA((len(pieces),))],
            compiler_params=params(16),
            cost_estimate=cost(0, nbytes),
        )(info, *pieces)

    def order(self, buckets):
        if self.high == 4 and buckets == 3:
            high = ((0, 2), (0, 1), (0, 3), (1, 2), (1, 1), (1, 3), (2, 2), (2, 1), (2, 3))
            low = ((0, 0), (1, 0), (0, 1), (0, 2), (2, 0), (0, 3), (1, 1), (1, 2), (1, 3), (2, 1), (2, 2), (2, 3))
            lanes = (1, 0, 1, 0, 1, 0, 0, 1, 0, 0, 1, 1, 0, 0, 1, 0, 1, 0, 1, 0, 0)
            highs, lows = iter(high), iter(low)
            steps = [(bool(lane), *next(highs if lane else lows)) for lane in lanes]
        else:
            keys = [0]
            while len(keys) < self.high:
                keys += [key | (self.high // (2 * len(keys))) for key in keys]
            steps = [(lane, index, key) for index in range(buckets) for key in keys for lane in (True, False)]
            steps = [step for step in steps if not step[0] or step[2]]
        queue = []
        for lane, index, key in steps:
            bit = key & -key
            if lane:
                queue.append(((index, key ^ bit, 0), (index, key, 0), bit))
            else:
                queue.append(((index, key, 0), (index, key, 1), 0))
        return queue

    def gather(self, locals_, window, hooks):
        got = {(index, 0, 0): local for index, local in enumerate(locals_)}
        queue = self.order(len(locals_))
        lasts = {index: max(n for n, item in enumerate(queue) if item[0][0] == index) for index in range(len(locals_))}
        hooks = {min(lasts[index] + lag, len(queue) - 2): (index, function) for index, lag, function in hooks}
        token = None
        for number, (source, target, bit) in enumerate(queue):
            values = got[source]
            if token is not None:
                values, token = after(values, token)[0], None
            if number >= window:
                old = queue[number - window][1]
                if old != source:
                    values, got[old] = lax.optimization_barrier((values, got[old]))
            got[target] = self.swap_high(values, bit) if bit else self.swap_low(values)
            if number in hooks:
                index, function = hooks[number]
                token = function(self.pieces(got, index))
        return [self.pieces(got, index) for index in range(len(locals_))]

    def pieces(self, got, index):
        return [got[index, key, side] for key in range(self.high) for side in range(2)]

    def split(self, values):
        values = values.reshape((self.high, 2) + values.shape[1:])
        return pick(values, 1 - self.mine_low, 1), pick(values, self.mine_low, 1)


class Sequence:
    def __init__(self, token):
        self.token = token

    def __call__(self, values):
        return after(values, self.token)[0]

    def mark(self, values):
        self.token = values
        return values


class Sums:
    def __init__(self, comm, sequence):
        self.comm, self.sequence = comm, sequence

    def low(self, *parts):
        parts = list(parts)
        parts[0] = self.sequence(parts[0])
        pairs = [self.comm.split(part) for part in parts]
        self.home = [pair[1] for pair in pairs]
        sent = self.sequence.mark(add(*[pair[0] for pair in pairs]))
        self.got = self.comm.swap_low(sent)
        self.bit = 0

    def step(self):
        comm = self.comm
        if not self.bit:
            total = add(self.sequence(self.got), *self.home)
            self.held = {key: pick(total, comm.mine_high ^ key, 0) for key in range(comm.high)}
            self.bit = 1
        else:
            self.receive()
            self.bit *= 2
        if self.bit >= comm.high:
            return False
        self.away = [key for key in self.held if key & self.bit]
        sent = self.sequence.mark(jnp.stack([self.held.pop(key) for key in self.away]))
        self.got = comm.swap_high(sent, self.bit)
        return True

    def receive(self):
        got = self.sequence(self.got)
        for index, key in enumerate(self.away):
            self.held[key ^ self.bit] = add(self.held[key ^ self.bit], got[index])

    def finish(self):
        while self.step():
            pass
        return self.sequence.mark(self.held[0])

    def over_replicas(self, values, bit):
        while bit < self.comm.replicas:
            values = add(values, self.comm.swap_replica(values, bit))
            bit *= 2
        return values


def add(*terms):
    return functools.reduce(jnp.add, [term.astype(F32) for term in terms]).astype(BF16)


def pick(values, index, axis):
    return lax.dynamic_index_in_dim(values, index, axis, keepdims=False)


def after(values, *tokens):
    return lax.optimization_barrier((values,) + tokens)


def per_device(
    sizes,
    tokens,
    encoded,
    lengths,
    cotangent,
    norm_self,
    q_self,
    k_self,
    v_self,
    o_self,
    bias_table,
    norm_cross,
    q_cross,
    k_cross,
    v_cross,
    o_cross,
    norm_ff,
    wi_gate,
    wi_up,
    wo_ff,
):
    count, replica_count = sizes
    comm = Links(count, replica_count)
    core_zero = comm.core == 0
    row_count, width = tokens.shape[1:]
    seq_count = lengths.shape[1]
    encoder = encoded[0].reshape(-1, width)
    enc_rows = encoder.shape[0]
    rows = q_self.shape[0]
    hidden_units = wi_gate.shape[1]
    down_rows = wo_ff.shape[0]
    half = width // 2
    info = jnp.concatenate(
        [jnp.stack([comm.core, comm.mine_high, comm.mine_low, comm.side]), lengths[0]]
    ).astype(jnp.int32)
    small = jnp.concatenate([norm_self, norm_cross, norm_ff, bias_table.reshape(-1)])
    small_count = small.shape[0]
    small = jnp.pad(small[None], ((0, 15), (0, width - small_count)))

    units = down_rows // 2
    side_zero = comm.side == 0
    wide = jnp.where(core_zero, wi_gate, wi_up).reshape(rows, count, 2, units)

    wide = pick(wide, comm.side, 2).reshape(rows, -1)
    down = pick(wo_ff.reshape(2, units, width), comm.side, 0)
    down = jnp.where(core_zero, down[:, :half], down[:, half:])
    down = down.reshape(4, units // 4, 3, PAIR).transpose(2, 1, 0, 3).reshape(rows, -1)
    feed_local = jnp.concatenate([wide, down], axis=1)
    first_local = jnp.concatenate(
        [jnp.where(core_zero, q_self, v_self), jnp.where(core_zero, k_self, o_self), small]
    )
    second_local = jnp.concatenate(
        [jnp.where(core_zero, q_cross, v_cross), jnp.where(core_zero, k_cross, o_cross)]
    )
    feed_pieces, first_pieces, second_pieces = comm.gather(
        [feed_local, first_local, second_local], 4, []
    )
    feed_one, first_mine = comm.collect(info, feed_pieces), comm.collect(info, first_pieces)
    feed_two = comm.swap_replica(feed_one, 2)
    feed_one_theirs = comm.swap_replica(feed_one, 1)
    first_theirs = comm.swap_replica(first_mine, 1)

    vectors = first_mine[:, 2 * rows, :small_count].astype(F32)
    gain_one = vectors[:, :rows].reshape(1, -1)
    gain_two = vectors[:, rows : 2 * rows].reshape(1, -1)
    gain_three = vectors[:, 2 * rows : 3 * rows].reshape(1, -1)
    table = vectors[:, 3 * rows :].reshape(-1, HEADS)
    turned = jnp.asarray((-np.arange(row_count)) % row_count, jnp.int32)
    bucket_hot = (
        bucket_of(turned)[:, None] == lax.iota(jnp.int32, table.shape[0])[None, :]
    ).astype(F32)
    line = jnp.dot(bucket_hot, table, precision=lax.Precision.HIGHEST).T
    line = jnp.pad(line, ((0, 16 - HEADS), (0, 0)))

    def shape(*dims, dtype=BF16):
        return jax.ShapeDtypeStruct(dims, dtype)

    act = shape(row_count, width)
    act_enc = shape(enc_rows, width)
    act32 = shape(row_count, width, dtype=F32)
    vec32 = shape(1, width, dtype=F32)
    weight_scratch = pltpu.VMEM((4, count, rows, width), BF16)
    sems = pltpu.SemaphoreType.DMA((4,))
    weight_bytes = 4 * count * rows * width * 2
    pair_flops = 2 * row_count * width * width
    attn_scratch = pltpu.VMEM((4, row_count, width), BF16)

    tokens_here = tokens[0]
    queries, keys, values, probs, attn_one, hidden_one = pl.pallas_call(
        functools.partial(self_forward, seq_count),
        out_shape=(act, act, act, shape(HEADS, row_count, row_count, dtype=F32), act, act32),
        in_specs=[SMEM, VMEM, VMEM, VMEM] + [ANY] * 2,
        out_specs=[VMEM] * 6,
        scratch_shapes=[weight_scratch, sems],
        compiler_params=params(),
        cost_estimate=cost(5 * pair_flops, weight_bytes),
    )(info, tokens_here, gain_one, line, first_mine, first_theirs)

    second_mine = comm.collect(info, second_pieces)
    second_theirs = comm.swap_replica(second_mine, 1)
    feed_two_theirs = comm.swap_replica(feed_two, 1)
    queries_c, keys_c, values_c, probs_c, attn_two, hidden_two, normed_three = pl.pallas_call(
        functools.partial(cross_forward, seq_count),
        out_shape=(act, act_enc, act_enc, shape(HEADS, row_count, enc_rows, dtype=F32), act, act32, act),
        in_specs=[SMEM, VMEM, VMEM, VMEM, VMEM] + [ANY] * 2,
        out_specs=[VMEM] * 7,
        scratch_shapes=[weight_scratch, sems],
        compiler_params=params(),
        cost_estimate=cost(5 * pair_flops, weight_bytes),
    )(info, hidden_one, gain_two, gain_three, encoder, second_mine, second_theirs)

    packed = shape(*feed_one.shape)
    feed_steps = pltpu.SemaphoreType.DMA((count, 4))
    feed_scratch = [pltpu.VMEM(feed_one.shape, BF16)] * 4 + [feed_steps, feed_steps]
    feed_cost = cost(9 * row_count * width * hidden_units, 12 * width * hidden_units)
    total, back, g_one, g_one_other = pl.pallas_call(
        functools.partial(feed_forward, False, seq_count),
        out_shape=(shape(2, row_count, half, dtype=F32), act32, packed, packed),
        in_specs=[SMEM, VMEM, VMEM, ANY, ANY],
        out_specs=[VMEM, VMEM, ANY, ANY],
        scratch_shapes=feed_scratch,
        compiler_params=params(),
        cost_estimate=feed_cost,
    )(info, normed_three, cotangent[0], feed_one, feed_one_theirs)
    mixed, grad_hidden_two, grad_norm_three, g_two, g_two_other = pl.pallas_call(
        functools.partial(feed_forward, True, seq_count),
        out_shape=(act, act32, vec32, packed, packed),
        in_specs=[SMEM, VMEM, VMEM, ANY, ANY] + [VMEM] * 4,
        out_specs=[VMEM] * 3 + [ANY] * 2,
        scratch_shapes=feed_scratch,
        compiler_params=params(),
        cost_estimate=feed_cost,
    )(info, normed_three, cotangent[0], feed_two, feed_two_theirs, hidden_two, gain_three, total, back)

    sequence = Sequence(grad_norm_three)
    one, two, second, first = (Sums(comm, sequence) for _ in range(4))
    one_got = comm.swap_replica(g_one_other, 1)
    two_got = comm.swap_replica(g_two_other, 1)
    one.low(g_one, one_got)
    grad_hidden_two = sequence(grad_hidden_two)

    grads = shape(count, rows, width)
    grads_half = shape(count // 2, rows, width)
    out_sems = pltpu.SemaphoreType.DMA((5,))
    grad_hidden_one, grad_encoder, grad_norm_two, *g_second = pl.pallas_call(
        functools.partial(cross_backward, seq_count),
        out_shape=(act32, shape(enc_rows, width, dtype=F32), vec32) + (grads,) * 3 + (grads_half,) * 2,
        in_specs=[SMEM] + [VMEM] * 9 + [ANY] * 2,
        out_specs=[VMEM] * 3 + [ANY] * 5,
        scratch_shapes=[weight_scratch, attn_scratch, weight_scratch, sems, out_sems],
        compiler_params=params(),
        cost_estimate=cost(10 * pair_flops, 2 * weight_bytes),
    )(
        info, grad_hidden_two, hidden_one, gain_two, encoder, queries_c, keys_c, values_c, probs_c, attn_two,
        second_mine, second_theirs,
    )
    def across(g_own, g_side, g_core, *g_far):
        from_far = [comm.swap_replica(part, 1) for part in g_far]
        from_core = comm.swap_replica(g_core, 1)

        def finish():
            from_far[0] = sequence(from_far[0])
            side = sequence.mark(add(jnp.concatenate(from_far), g_side))
            return g_own, from_core, comm.swap_replica(side, 2)

        return finish

    sequence.mark(grad_norm_two)
    two.low(g_two, two_got)
    second_parts = across(*g_second)()
    grad_hidden_one = sequence(grad_hidden_one)

    grad_inputs, grad_norm_one, grad_line, *g_first = pl.pallas_call(
        functools.partial(self_backward, seq_count),
        out_shape=(act32, vec32, shape(16, row_count, dtype=F32)) + (grads,) * 3 + (grads_half,) * 2,
        in_specs=[SMEM] + [VMEM] * 8 + [ANY] * 2,
        out_specs=[VMEM] * 3 + [ANY] * 5,
        scratch_shapes=[weight_scratch, attn_scratch, weight_scratch, sems, out_sems],
        compiler_params=params(),
        cost_estimate=cost(10 * pair_flops, 2 * weight_bytes),
    )(
        info, grad_hidden_one, tokens_here, gain_one, queries, keys, values, probs, attn_one,
        first_mine, first_theirs,
    )
    sequence.mark(grad_norm_one)
    first_across = across(*g_first)
    one.step()
    first_parts = first_across()
    second.low(*second_parts)
    grad_table = jnp.dot(grad_line[:HEADS], bucket_hot, precision=lax.Precision.HIGHEST).T
    table_row = jnp.pad(grad_table.reshape(1, -1), ((0, 0), (0, width - grad_table.size)))
    vectors = jnp.concatenate([grad_norm_one, grad_norm_two, grad_norm_three, table_row])
    steps = [("replica", 1 << k) for k in range(replica_count.bit_length() - 1)]
    steps += [("fsdp", 1 << k) for k in range(count.bit_length() - 1)]

    def small_step():
        axis, bit = steps.pop(0)
        size = replica_count if axis == "replica" else count
        return lax.ppermute(sequence(vectors), axis, [(i, i ^ bit) for i in range(size)])

    def small_sum(got):
        return vectors + sequence(got)

    got = small_step()
    one.step()
    two.step()
    vectors = small_sum(got)
    got = small_step()
    second.step()
    first.low(*first_parts)
    vectors = small_sum(got)
    got = small_step()
    one_part = one.finish()
    two.step()
    second.step()
    vectors = small_sum(got)
    got = small_step()
    first.step()
    vectors = small_sum(got)
    got = small_step()
    two_part = two.finish()
    one_cross, two_cross = comm.swap_replica(two_part, 2), comm.swap_replica(one_part, 2)
    first.step()
    second_sum = second.over_replicas(second.finish(), 4)
    second_cross, second_core = comm.swap_replica(second_sum, 2), comm.swap_replica(second_sum, 1)
    one_sum = one.over_replicas(add(one_part, sequence(one_cross)), 4)
    two_sum = two.over_replicas(add(two_part, two_cross), 4)
    sequence.mark(two_sum)
    there = comm.swap_replica(one_sum, 1), comm.swap_replica(two_sum, 1)
    vectors = small_sum(got)
    while steps:
        vectors = small_sum(small_step())
    first_sum = first.over_replicas(first.finish(), 4)
    first_cross, first_core = comm.swap_replica(first_sum, 2), comm.swap_replica(first_sum, 1)
    second_far = comm.swap_replica(second_cross, 1)
    first_far = None

    full = jax.ShapeDtypeStruct((rows, width), F32)

    def four(*arrays):
        return pl.pallas_call(
            finish_quarters,
            out_shape=(full,) * 4,
            in_specs=[SMEM] + [VMEM] * 4,
            out_specs=[VMEM] * 4,
            compiler_params=params(16),
            cost_estimate=cost(0, 24 * rows * width),
        )(info, *arrays)

    owned = lax.dynamic_slice(vectors, (0, comm.place * rows), (3, rows))
    table_size = bias_table.size
    owned_table = lax.dynamic_slice(vectors[3], (comm.place * table_size,), (table_size,))

    second = four(second_sum, second_cross, second_core, second_far)
    if units % PAIR == 0:
        grad_gate, grad_up, grad_down = pl.pallas_call(
            finish_feed,
            out_shape=(
                shape(rows, hidden_units, dtype=F32), shape(rows, hidden_units, dtype=F32),
                shape(down_rows, width, dtype=F32),
            ),
            in_specs=[SMEM] + [VMEM] * 4,
            out_specs=[VMEM] * 3,
            compiler_params=params(16),
            cost_estimate=cost(0, 36 * rows * hidden_units),
        )(info, one_sum, two_sum, *there)
    else:
        def by_side(one, two):
            return jnp.where(side_zero, one, two), jnp.where(side_zero, two, one)

        here, there = by_side(one_sum, two_sum), by_side(*there)
        wide_units = hidden_units // 2

        def wide_grad(parts):
            parts = [part[:, :wide_units].reshape(rows, count, 1, units) for part in parts]
            return jnp.concatenate(parts, axis=2).reshape(rows, hidden_units).astype(F32)

        def down_grad(parts):
            parts = [
                part[:, wide_units:].reshape(3, units // 4, 4, PAIR).transpose(2, 1, 0, 3).reshape(units, half)
                for part in parts
            ]
            return jnp.concatenate(parts, axis=0)

        low = [jnp.where(core_zero, one, two) for one, two in zip(here, there)]
        high = [jnp.where(core_zero, two, one) for one, two in zip(here, there)]
        grad_down = jnp.concatenate([down_grad(low), down_grad(high)], axis=1).astype(F32)
        grad_gate, grad_up = wide_grad(low), wide_grad(high)
    first_far = comm.swap_replica(after(first_cross, grad_gate, grad_up, grad_down, *second)[0], 1)
    first = four(first_sum, first_cross, first_core, first_far)
    return (
        mixed[None],
        grad_inputs[None],
        grad_encoder.reshape(encoded.shape),
        owned[0],
        first[0],
        first[1],
        first[2],
        first[3],
        owned_table.reshape(bias_table.shape),
        owned[1],
        second[0],
        second[1],
        second[2],
        second[3],
        owned[2],
        grad_gate,
        grad_up,
        grad_down,
    )


def solution(mesh):
    slots = P(("replica", "fsdp"), None, None)
    slots_four = P(("replica", "fsdp"), None, None, None)
    vector, matrix = P("fsdp"), P("fsdp", None)
    weights = (
        (vector,) + (matrix,) * 5 + (vector,) + (matrix,) * 4 + (vector,) + (matrix,) * 3
    )
    return jax.shard_map(
        functools.partial(per_device, (mesh.shape["fsdp"], mesh.shape["replica"])),
        mesh=mesh,
        in_specs=(slots, slots_four, P(("replica", "fsdp"), None), slots) + weights,
        out_specs=(slots, slots, slots_four) + weights,
        check_vma=False,
    )
```
